256 devices in a mesh: dp: 4 (over y), bal: 64 (over z, x, core).
Axes of the slice: x: 4, y: 4, z: 8, core: 2. Of those that a mesh axis runs over, the one named last changes fastest.
Arguments:
- queries: bfloat16 [131072, 1024], P(('dp', 'bal')), may hold values from -6 to 6
- keys: bfloat16 [131072, 1024], P(('dp', 'bal')), may hold values from -6 to 6
- values: bfloat16 [131072, 1024], P(('dp', 'bal')), may hold values from -6 to 6
- gates: bfloat16 [131072, 1024], P(('dp', 'bal')), may hold values from -24 to 24
- cotangent: bfloat16 [131072, 1024], P(('dp', 'bal')), may hold values from -6 to 6
- hist_len: int32 [256, 8], P(('dp', 'bal')), may hold values from 1 to 256, 512 in all within a row
- token_owner: int32 [131072], P(('dp', 'bal')), may hold values from 0 to 63, as said below
- token_row: int32 [131072], P(('dp', 'bal')), may hold values from 0 to 511
- w_out: bfloat16 [1024, 1024], P('dp'), may hold values from -0.1875 to 0.1875
Outputs:
- output: bfloat16 [131072, 1024], P(('dp', 'bal'))
- grad_queries: bfloat16 [131072, 1024], P(('dp', 'bal'))
- grad_keys: bfloat16 [131072, 1024], P(('dp', 'bal'))
- grad_values: bfloat16 [131072, 1024], P(('dp', 'bal'))
- grad_gates: bfloat16 [131072, 1024], P(('dp', 'bal'))
- grad_weight: float32 [1024, 1024], P('dp')
The draws below stay inside these ranges and needn't reach their ends.
Inputs may be any that keep to these rules, and one draw needn't show every extreme that they name: Within each user group, every owner receives exactly 512 tokens, and the pairs (token_owner, token_row) are all different. The 512 tokens of one source device hold at most 16 tokens for one owner, and every source device holds exactly 16 for some owner.
All inputs are finite; a program needn't handle non-finite values.
Results may differ from the reference program's by a relative error of at most 0.014.
Values may be sent and summed in bfloat16 or wider, within the bound.
A program may use at most 128 MiB of HBM per device.

```python
import math
import jax
import jax.numpy as jnp
import numpy as np
from jax import lax

D = 1024
HEAD = 128
TOK_DEV = 512
USERS_OWN = 8
MAXLEN = 256
TOKENS = 131072
N_DP = 4
N_BAL = 64


def route_tables(key):
    peer_share = TOK_DEV // N_BAL
    group_total = N_BAL * TOK_DEV

    def one_group(group_key):
        key_load, key_shift, key_rows, key_order = jax.random.split(group_key, 4)
        offset = jax.random.randint(key_load, (N_BAL // 2,), -peer_share, peer_share + 1, dtype=jnp.int32)
        offset = offset.at[0].set(peer_share)
        loads = jnp.concatenate([peer_share + offset, peer_share - offset])
        rotation = jax.random.permutation(key_shift, N_BAL).astype(jnp.int32)
        senders = jnp.arange(N_BAL, dtype=jnp.int32)
        targets = (senders[:, None] + rotation[None, :]) % N_BAL
        counts = jnp.zeros((N_BAL, N_BAL), jnp.int32).at[senders[:, None], targets].set(jnp.broadcast_to(loads[None, :], (N_BAL, N_BAL)))
        upper = jnp.cumsum(counts, axis=0)
        row_ids = jnp.arange(TOK_DEV, dtype=jnp.int32)
        sender_of = jnp.sum((upper[:, :, None] <= row_ids[None, None, :]).astype(jnp.int32), axis=0)
        row_keys = jax.random.split(key_rows, N_BAL)

        def shuffle_one(row_key):
            return jax.random.permutation(row_key, TOK_DEV).astype(jnp.int32)
        shuffle = jax.vmap(shuffle_one)(row_keys)
        sender_of = jnp.take_along_axis(sender_of, shuffle, axis=1)
        ranks = jax.random.permutation(key_order, group_total).astype(jnp.int32)
        order = jnp.argsort(sender_of.reshape(-1) * group_total + ranks, stable=True)
        return order.astype(jnp.int32)
    group_keys = jax.random.split(key, N_DP)
    return jax.vmap(one_group)(group_keys).reshape(-1)


def draw_token_owner(key, part):
    order = route_tables(key)
    return (order // TOK_DEV).astype(jnp.int32)


def draw_token_row(key, part):
    order = route_tables(key)
    return (order % TOK_DEV).astype(jnp.int32)


def raised(entries, own_key, source, target, shards_of, factor):
    def block_of(dim):
        return (jnp.arange(entries.shape[dim]) // (entries.shape[dim] // shards_of)).reshape((-1,) + (1,) * (entries.ndim - 1 - dim))

    near = jax.random.permutation(own_key, shards_of)[block_of(target)]
    second = (block_of(target) + shards_of // 2) % shards_of
    return jnp.where((block_of(source) == near) | (block_of(source) == second), factor * entries, entries)


def shard_levels(stream_key, extent, cuts, smallest, high):
    loudness, own = 1.0, jax.random.fold_in(stream_key, 6)
    for axis_at, blocks in cuts:
        steps = jnp.exp(jax.random.uniform(jax.random.fold_in(own, axis_at), (blocks,), jnp.float32, smallest / len(cuts), high / len(cuts)))
        loudness = loudness * jnp.repeat(steps, extent[axis_at] // blocks).reshape([-1 if axis == axis_at else 1 for axis in range(len(extent))])
    return loudness


def split_up(count, total, reach, skew):
    weights = [(1 << 20) // math.isqrt(standing ** skew) + 1 for standing in range(2, count + 1)]
    rest, holding = total - reach - (count - 1), [1] * (count - 1)
    while rest > 0:
        movable = [i for i in range(count - 1) if holding[i] < reach]
        whole, budget = sum([weights[i] for i in movable]), rest
        for i in movable:
            more = min(reach - holding[i], max(1, budget * weights[i] // whole), rest)
            holding[i] = holding[i] + more
            rest = rest - more
    return np.array([reach] + holding)


def ragged(key, amount, total, bound, skew):
    if amount == 2:
        one = jax.random.randint(key, (), max(1, total - bound), min(bound, total - 1) + 1)
        return jnp.stack([one, total - one])
    sizes = jnp.asarray(split_up(amount, total, bound, skew), jnp.int32)
    couples = (amount - 1) // 2
    donor, taker = sizes[1:1 + 2 * couples:2], sizes[2:2 + 2 * couples:2]
    slack = jnp.minimum(donor - 1, bound - taker)
    moved = jax.random.randint(jax.random.fold_in(key, 1), (couples,), 0, 1 << 20) % (slack + 1)
    sizes = sizes.at[1:1 + 2 * couples:2].set(donor - moved).at[2:2 + 2 * couples:2].set(taker + moved)
    return sizes[jax.random.permutation(jax.random.fold_in(key, 2), amount)]


def bell_draw(own_key, dims, width, most, pieces=(), kind=jnp.bfloat16):
    values = jax.random.normal(own_key, dims, jnp.float32) * width
    if len(pieces) > 0:
        values = shard_levels(own_key, dims, pieces, -0.22, 0.18) * values
    return jnp.clip(values, min=-most, max=most).astype(kind)


def bell_draw_with(key, extent, width, limit, cuts, heavy, held_as=jnp.bfloat16):
    drawn = width * jax.random.normal(key, extent, jnp.float32)
    if cuts:
        drawn = drawn * shard_levels(key, extent, cuts, -0.22, 0.18)
    return jnp.clip(raised(drawn, jax.random.fold_in(key, 3), *heavy), -limit, limit).astype(held_as)


def setup_inputs(seed: int = 0) -> dict:
    arg_keys = jax.random.split(jax.random.key(seed), 10)
    queries = bell_draw(arg_keys[0], (TOKENS, D), 1.0, 6.0, ((0, 256),))
    keys = bell_draw(arg_keys[1], (TOKENS, D), 1.0, 6.0, ((0, 256),))
    values = bell_draw(arg_keys[2], (TOKENS, D), 1.0, 6.0, ((0, 256),))
    gates = bell_draw_with(arg_keys[3], (TOKENS, D), 1.0, 24.0, ((0, 256),), (0, 1, 256, 6.0))
    cotangent = bell_draw(arg_keys[4], (TOKENS, D), 1.0, 6.0, ((0, 256),))
    hist_len = jax.vmap(lambda own: ragged(own, USERS_OWN, TOK_DEV, MAXLEN, 2))(jax.random.split(arg_keys[5], (N_DP * N_BAL))).reshape((N_DP * N_BAL, USERS_OWN)).astype(jnp.int32)
    token_owner = draw_token_owner(jax.random.fold_in(arg_keys[9], 71), 0)
    token_row = draw_token_row(jax.random.fold_in(arg_keys[9], 71), 0)
    w_out = bell_draw(arg_keys[8], (D, D), D ** -0.5, 0.1875, ((0, 4),))
    return dict(queries=queries, keys=keys, values=values, gates=gates, cotangent=cotangent, hist_len=hist_len, token_owner=token_owner, token_row=token_row, w_out=w_out)


EPSILON = 1e-05

def history_mask(lengths, row_count):
    history_end = jnp.cumsum(lengths)
    positions = jnp.arange(row_count, dtype=jnp.int32)
    history_id = lax.optimization_barrier(jnp.sum((positions[:, None] >= history_end[None, :]).astype(jnp.int32), axis=1))
    return (history_id[:, None] == history_id[None, :]) & (positions[:, None] >= positions[None, :])

def split_heads(tensor):
    return tensor.reshape(tensor.shape[0], -1, HEAD).astype(jnp.float32)

def rounded(tensor):
    return lax.optimization_barrier(tensor.astype(jnp.bfloat16)).astype(jnp.float32)

def scores_of(own_q, own_k):
    return jnp.einsum('ihe,jhe->hij', split_heads(own_q), split_heads(own_k)) / math.sqrt(HEAD)

def owner_forward(own_q, own_k, own_v, allowed):
    scores = scores_of(own_q, own_k)
    weights = rounded(jnp.where(allowed[None], jax.nn.silu(scores), 0.0))
    attended = jnp.einsum('hij,jhe->ihe', weights, split_heads(own_v))
    return attended.reshape(own_q.shape[0], -1).astype(jnp.bfloat16)

def owner_backward(own_q, own_k, own_v, allowed, grad_own):
    row_count = own_q.shape[0]
    scores = scores_of(own_q, own_k)
    sigmoid_val = jax.nn.sigmoid(scores)
    weights = rounded(jnp.where(allowed[None], jax.nn.silu(scores), 0.0))
    grad_heads = split_heads(grad_own)
    grad_probs = jnp.einsum('ihe,jhe->hij', grad_heads, split_heads(own_v))
    grad_scores = jnp.where(allowed[None], grad_probs * sigmoid_val * (1.0 + scores * (1.0 - sigmoid_val)), 0.0) / math.sqrt(HEAD)
    grad_scores = rounded(grad_scores)
    grad_v = jnp.einsum('hij,ihe->jhe', weights, grad_heads).reshape(row_count, -1).astype(jnp.bfloat16)
    grad_q = jnp.einsum('hij,jhe->ihe', grad_scores, split_heads(own_k)).reshape(row_count, -1).astype(jnp.bfloat16)
    grad_k = jnp.einsum('hij,ihe->jhe', grad_scores, split_heads(own_q)).reshape(row_count, -1).astype(jnp.bfloat16)
    return (grad_q, grad_k, grad_v)

def normalize(attended):
    wide = attended.astype(jnp.float32)
    centered = wide - lax.optimization_barrier(jnp.mean(wide, axis=-1, keepdims=True))
    inverse = lax.rsqrt(lax.optimization_barrier(jnp.mean(centered * centered, axis=-1, keepdims=True)) + EPSILON)
    return (centered * inverse, inverse)

def gating_backward(grad_hidden, normed, inverse, gates):
    grad_gates = (grad_hidden * normed).astype(jnp.bfloat16)
    grad_normed = grad_hidden * gates.astype(jnp.float32)
    mean_grad = lax.optimization_barrier(jnp.mean(grad_normed, axis=-1, keepdims=True))
    mean_cross = lax.optimization_barrier(jnp.mean(grad_normed * normed, axis=-1, keepdims=True))
    grad_attended = (grad_normed - mean_grad - normed * mean_cross) * inverse
    return (grad_gates, grad_attended.astype(jnp.bfloat16))

def reference(queries, keys, values, gates, cotangent, hist_len, token_owner, token_row, w_out):
    token_count = queries.shape[0]
    group_size = N_BAL * TOK_DEV
    landing = jnp.arange(token_count, dtype=jnp.int32) // group_size * group_size + token_owner * TOK_DEV + token_row

    def to_owner(tensor):
        return jnp.zeros_like(tensor).at[landing].set(tensor).reshape(-1, TOK_DEV, tensor.shape[1])

    def from_owner(tensor):
        return tensor.reshape(token_count, -1)[landing]
    own_q = to_owner(queries)
    own_k = to_owner(keys)
    own_v = to_owner(values)

    def forward_one(owner_item):
        return owner_forward(owner_item[0], owner_item[1], owner_item[2], history_mask(owner_item[3], TOK_DEV))
    attended = from_owner(lax.map(forward_one, (own_q, own_k, own_v, hist_len)))
    normed, inverse = normalize(attended)
    gated = (normed * gates.astype(jnp.float32)).astype(jnp.bfloat16)
    output = jnp.dot(gated, w_out, preferred_element_type=jnp.float32).astype(jnp.bfloat16)
    grad_hidden = jnp.dot(cotangent, w_out.T, preferred_element_type=jnp.float32)
    grad_weight = jnp.dot(gated.T, cotangent, preferred_element_type=jnp.float32)
    grad_gates, grad_attended = gating_backward(grad_hidden, normed, inverse, gates)
    grad_own = to_owner(grad_attended)

    def backward_one(owner_item):
        return owner_backward(owner_item[0], owner_item[1], owner_item[2], history_mask(owner_item[3], TOK_DEV), owner_item[4])
    grads = lax.map(backward_one, (own_q, own_k, own_v, hist_len, grad_own))
    return (output, from_owner(grads[0]), from_owner(grads[1]), from_owner(grads[2]), grad_gates, grad_weight)
```

```python
import functools
import math

import jax
import jax.numpy as jnp
from jax import lax
from jax.experimental import pallas as pl
from jax.experimental.pallas import tpu as pltpu
from jax.sharding import PartitionSpec as P

HEAD = 128
EPSILON = 1e-05
SLOTS = 16
MESH = pl.DeviceIdType.MESH
F32 = jnp.float32
BF16 = jnp.bfloat16
META = 768


def nn(a, b):
    return lax.dot_general(a, b, (((1,), (0,)), ((), ())), preferred_element_type=F32)


def nt(a, b):
    return lax.dot_general(a, b, (((1,), (1,)), ((), ())), preferred_element_type=F32)


def tn(a, b):
    return lax.dot_general(a, b, (((0,), (0,)), ((), ())), preferred_element_type=F32)


def block_wait(ref, sem):
    pltpu.make_async_copy(ref, ref, sem).wait()


def kernel(
    nz, npeer, ny,
    q_ref, k_ref, v_ref, gates_ref, cot_ref, meta_ref, w_ref,
    out_ref, gq_ref, gk_ref, gv_ref, gg_ref, gw_ref, xback,
    onehot_src, onehot_own, zbuf, xsend, xrecv, own, att_own, wfull, att_full,
    metaz, tsend, trecv, stat_s, stat_r, stat_f,
    dw_send, dw_recv, r1_send, r1_recv, r2_send, r2_recv, gz, gp,
    loc, zin_s, zin_r, xin_s, xin_r, xo_s, xo_r, zo_s, zo_r,
    m_s, m_r, t_s, t_r, w_s, w_r, sa_s, sa_r, sb_s, sb_r,
    dy_s, dy_r, dp_s, dp_r, dz_s, dz_r, az_s, az_r, ap_s, ap_r,
):
    y = lax.axis_index("dp")
    b = lax.axis_index("bal")
    z = b // npeer
    p = lax.rem(b, npeer)
    rows = q_ref.shape[0]
    slots = npeer * nz * SLOTS
    scale = 1.0 / math.sqrt(HEAD)

    def zpeer(d):
        return lax.rem(z + d, nz)

    def ppeer(d):
        return lax.rem(p + d, npeer)

    def ypeer(d):
        return lax.rem(y + d, ny)

    def zdev(at):
        return (y, at * npeer + p)

    def pdev(at):
        return (y, z * npeer + at)

    def ydev(at):
        return (at, b)

    def columns(at):
        return pl.ds(pl.multiple_of(at * HEAD, HEAD), HEAD)

    def remote(src, dst, ssem, rsem, device):
        copy = pltpu.make_async_remote_copy(
            src_ref=src, dst_ref=dst, send_sem=ssem, recv_sem=rsem,
            device_id=device, device_id_type=MESH,
        )
        copy.start()
        return copy

    barrier = pltpu.get_barrier_semaphore()
    for d in range(1, nz):
        pl.semaphore_signal(barrier, inc=1, device_id=zdev(zpeer(d)), device_id_type=MESH)
    for d in range(1, npeer):
        pl.semaphore_signal(barrier, inc=1, device_id=pdev(ppeer(d)), device_id_type=MESH)
    for d in range(1, ny):
        pl.semaphore_signal(barrier, inc=1, device_id=ydev(ypeer(d)), device_id_type=MESH)
    pl.semaphore_wait(barrier, nz + npeer + ny - 3)

    meta_copies = [
        remote(meta_ref, metaz.at[z], m_s.at[d], m_r.at[d], zdev(zpeer(d))) for d in range(1, nz)
    ]
    w_copies = [
        remote(w_ref, wfull.at[y], w_s.at[d], w_r.at[d], ydev(ypeer(d))) for d in range(1, ny)
    ]
    w_local = pltpu.make_async_copy(w_ref, wfull.at[y], loc.at[0])
    w_local.start()

    def z_in(u, src):
        pltpu.make_async_copy(src.at[:, columns(z)], zbuf.at[u, z], zin_r.at[u, 0]).start()
        return [
            remote(
                src.at[:, columns(zpeer(d))], zbuf.at[u, z], zin_s.at[u, d], zin_r.at[u, d],
                zdev(zpeer(d)),
            )
            for d in range(1, nz)
        ]

    zin_copies = [z_in(0, q_ref), z_in(1, k_ref), z_in(2, v_ref)]
    metaz[z] = meta_ref[...]

    w_local.wait()
    for copy in w_copies:
        copy.wait_recv()
    wrows = wfull.shape[1]

    def dz_block(i, _):
        r = pl.ds(pl.multiple_of(i * 128, 128), 128)
        cot = cot_ref[r, :]
        for j in range(ny):
            c = slice(j * wrows, (j + 1) * wrows)
            gg_ref[r, c] = (nt(cot, wfull[j]) * gates_ref[r, c].astype(F32)).astype(BF16)
        return 0

    lax.fori_loop(0, rows // 128, dz_block, 0)
    zin_copies.append(z_in(3, gg_ref))

    for copy in meta_copies:
        copy.wait_recv()
    for at in range(npeer):
        tsend[at] = metaz[:, at, 512:640]
    t_copies = [
        remote(tsend.at[ppeer(d)], trecv.at[p], t_s.at[d], t_r.at[d], pdev(ppeer(d)))
        for d in range(1, npeer)
    ]
    trecv[p] = tsend[p]

    def build_src(i, _):
        slot = metaz[i, 0:1, 0:512]
        for c in range(slots // 128):
            ids = lax.broadcasted_iota(jnp.int32, (128, rows), 0) + c * 128
            onehot_src[i, c * 128 : (c + 1) * 128, :] = jnp.where(ids == slot, 1.0, 0.0).astype(BF16)
        return 0

    lax.fori_loop(0, nz, build_src, 0)

    def pack_in(u):
        def step(d, _):
            at = lax.rem(z - d + nz, nz)
            block_wait(zbuf.at[u, at], zin_r.at[u, d])
            moved = nn(onehot_src[at], zbuf[u, at]).astype(BF16)
            xsend[u, :, :, at] = moved.reshape(npeer, nz, SLOTS, HEAD)
            return 0

        lax.fori_loop(0, nz, step, 0)
        pltpu.make_async_copy(xsend.at[u, p], xrecv.at[u, p], xin_r.at[u, 0]).start()
        return [
            remote(
                xsend.at[u, ppeer(d)], xrecv.at[u, p], xin_s.at[u, d], xin_r.at[u, d],
                pdev(ppeer(d)),
            )
            for d in range(1, npeer)
        ]

    def unpack_in(u):
        for d in range(npeer):
            at = lax.rem(p - d + npeer, npeer)
            block_wait(xrecv.at[u, at], xin_r.at[u, d])

        def step(o, _):
            own[u, o] = nn(onehot_own[o], xrecv[u, :, o].reshape(slots, HEAD)).astype(BF16)
            return 0

        lax.fori_loop(0, nz, step, 0)

    xin_copies = [pack_in(0)]

    for copy in t_copies:
        copy.wait_recv()
    group = npeer * nz

    def build_own(o, _):
        table = trecv[...].reshape(group, 128)
        high = (table // 16).astype(F32).astype(BF16)
        low = (table % 16).astype(F32).astype(BF16)
        lane = lax.broadcasted_iota(jnp.int32, (128, slots), 1)
        take = lax.broadcasted_iota(jnp.int32, (128, slots), 0)
        pick = jnp.where(take == o * SLOTS + lane % SLOTS, 1.0, 0.0).astype(BF16)
        spread = nn(high, pick) * 16.0 + nn(low, pick)
        which = lax.broadcasted_iota(jnp.int32, (group, slots), 0)
        at = lax.broadcasted_iota(jnp.int32, (group, slots), 1) // SLOTS
        row = jnp.sum(jnp.where(which == at, spread, 0.0), axis=0, keepdims=True).astype(jnp.int32)
        for c in range(rows // 128):
            ids = lax.broadcasted_iota(jnp.int32, (128, slots), 0) + c * 128
            onehot_own[o, c * 128 : (c + 1) * 128, :] = jnp.where(ids == row, 1.0, 0.0).astype(BF16)
        return 0

    lax.fori_loop(0, nz, build_own, 0)

    xin_copies.append(pack_in(1))
    unpack_in(0)
    xin_copies.append(pack_in(2))
    unpack_in(1)
    xin_copies.append(pack_in(3))
    unpack_in(2)

    def allowed_of(o):
        lengths = metaz[o, 0:1, 640:768]
        line = lax.broadcasted_iota(jnp.int32, (rows, 1), 0)
        end = jnp.zeros((1, 1), jnp.int32)
        start = jnp.zeros((rows, 1), jnp.int32)
        for h in range(8):
            length = lengths[:, h : h + 1]
            end = end + length
            start = start + jnp.where(line >= end, length, 0)
        i = lax.broadcasted_iota(jnp.int32, (rows, rows), 0)
        j = lax.broadcasted_iota(jnp.int32, (rows, rows), 1)
        return (j <= i) & (j >= start)

    for copy in xin_copies[0]:
        copy.wait_send()

    def forward(o, _):
        scores = nt(own[0, o], own[1, o]) * scale
        sig = 0.5 * jnp.tanh(0.5 * scores) + 0.5
        weights = jnp.where(allowed_of(o), scores * sig, 0.0).astype(BF16)
        att = nn(weights, own[2, o]).astype(BF16)
        att_own[o] = att
        moved = tn(att, onehot_own[o]).T.astype(BF16)
        xsend[0, :, o] = moved.reshape(npeer, nz, SLOTS, HEAD)
        return 0

    lax.fori_loop(0, nz, forward, 0)

    def x_out(u):
        pltpu.make_async_copy(xsend.at[u, p], xback.at[u, p], xo_r.at[u, 0]).start()
        return [
            remote(
                xsend.at[u, ppeer(d)], xback.at[u, p], xo_s.at[u, d], xo_r.at[u, d],
                pdev(ppeer(d)),
            )
            for d in range(1, npeer)
        ]

    xo_copies = [x_out(0)]

    unpack_in(3)

    def stats(o, _):
        att = att_own[o].astype(F32)
        dz = own[3, o].astype(F32)
        mean = jnp.sum(att, axis=1, keepdims=True) * (1.0 / HEAD)
        cent = att - mean
        second = jnp.sum(cent * cent, axis=1, keepdims=True)
        total = jnp.sum(dz, axis=1, keepdims=True)
        cross = jnp.sum(dz * cent, axis=1, keepdims=True)
        lane = lax.broadcasted_iota(jnp.int32, (rows, HEAD), 1)
        table = jnp.where(
            lane == 0, mean, jnp.where(lane == 1, second, jnp.where(lane == 2, total, cross))
        )
        stat_s[o] = table.T[0:8, :]
        return 0

    lax.fori_loop(0, nz, stats, 0)
    sa_copies = [
        remote(stat_s.at[zpeer(d)], stat_r.at[z], sa_s.at[d], sa_r.at[d], zdev(zpeer(d)))
        for d in range(1, nz)
    ]
    stat_r[z] = stat_s[z]
    for copy in sa_copies:
        copy.wait_recv()
    features = float(nz * HEAD)
    got = stat_r[...]
    means, seconds, totals, crosses = [got[:, i : i + 1, :] for i in range(4)]
    mean = jnp.sum(means, axis=0) * (1.0 / nz)
    shift = means - mean[None]
    var = (jnp.sum(seconds, axis=0) + HEAD * jnp.sum(shift * shift, axis=0)) / features
    inverse = lax.rsqrt(var + EPSILON)
    mean_grad = jnp.sum(totals, axis=0) / features
    mean_cross = jnp.sum(crosses + shift * totals, axis=0) * inverse / features
    stat_f[z] = jnp.concatenate([mean, inverse, mean_grad, mean_cross] * 2, axis=0)
    sb_copies = [
        remote(stat_f.at[z], stat_f.at[z], sb_s.at[d], sb_r.at[d], zdev(zpeer(d)))
        for d in range(1, nz)
    ]
    for u in (1, 2, 3):
        for copy in xin_copies[u]:
            copy.wait_send()
    for copy in sb_copies:
        copy.wait_recv()

    def backward(o, _):
        full = jnp.concatenate([stat_f[o]] * (HEAD // 8), axis=0).T
        mean, inverse = full[:, 0:1], full[:, 1:2]
        mean_grad, mean_cross = full[:, 2:3], full[:, 3:4]
        normed = (att_own[o].astype(F32) - mean) * inverse
        grad = (own[3, o].astype(F32) - mean_grad - normed * mean_cross) * inverse
        grad = grad.astype(BF16)
        allowed = allowed_of(o)
        q, k, v = own[0, o], own[1, o], own[2, o]
        scores = nt(q, k) * scale
        sig = 0.5 * jnp.tanh(0.5 * scores) + 0.5
        value = scores * sig
        weights = jnp.where(allowed, value, 0.0).astype(BF16)
        probs = nt(grad, v)
        slope = sig + value * (1.0 - sig)
        gs = jnp.where(allowed, probs * slope * scale, 0.0).astype(BF16)
        gq_t = nn(gs, k).astype(BF16)
        gk_t = tn(q, gs).astype(BF16)
        gv_t = tn(grad, weights).astype(BF16)
        spots = onehot_own[o]
        xsend[1, :, o] = tn(gq_t, spots).T.astype(BF16).reshape(npeer, nz, SLOTS, HEAD)
        xsend[2, :, o] = nn(gk_t, spots).T.astype(BF16).reshape(npeer, nz, SLOTS, HEAD)
        xsend[3, :, o] = nn(gv_t, spots).T.astype(BF16).reshape(npeer, nz, SLOTS, HEAD)
        return 0

    lax.fori_loop(0, nz, backward, 0)
    xo_copies += [x_out(1), x_out(2), x_out(3)]
    for u in range(4):
        for copy in zin_copies[u]:
            copy.wait_send()

    def back(u, dst):
        for d in range(npeer):
            at = lax.rem(p - d + npeer, npeer)
            block_wait(xback.at[u, at], xo_r.at[u, d])
        stage = pltpu.make_async_copy(xback.at[u], xrecv.at[u], loc.at[1 + u])
        stage.start()
        stage.wait()

        def tokens(at):
            got = xrecv[u, :, :, at].reshape(slots, HEAD)
            zbuf[u, at] = tn(got, onehot_src[at]).T.astype(BF16)

        def step(d, _):
            at = lax.rem(z + d, nz)
            tokens(at)
            remote(
                zbuf.at[u, at], dst.at[:, columns(z)], zo_s.at[u, d], zo_r.at[u, d], zdev(at)
            )
            return 0

        lax.fori_loop(1, nz, step, 0)
        tokens(z)
        pltpu.make_async_copy(zbuf.at[u, z], dst.at[:, columns(z)], zo_r.at[u, 0]).start()

    def back_wait(u, dst):
        for d in range(nz):
            at = lax.rem(z - d + nz, nz)
            block_wait(dst.at[:, columns(at)], zo_r.at[u, d])

    back(0, att_full)
    back(1, gq_ref)

    back_wait(0, att_full)

    def final_block(i, _):
        r = pl.ds(pl.multiple_of(i * 128, 128), 128)
        att = att_full[r, :].astype(F32)
        cent = att - jnp.mean(att, axis=1, keepdims=True)
        inv = lax.rsqrt(jnp.mean(cent * cent, axis=1, keepdims=True) + EPSILON)
        normed = cent * inv
        gated = (normed * gates_ref[r, :].astype(F32)).astype(BF16)
        att_full[r, :] = gated
        cot = cot_ref[r, :]
        acc = None
        for j in range(ny):
            c = slice(j * wrows, (j + 1) * wrows)
            gg_ref[r, c] = (nt(cot, wfull[j]) * normed[:, c]).astype(BF16)
            part = nn(gated[:, c], wfull[j])
            acc = part if acc is None else acc + part
        out_ref[r, :] = acc.astype(BF16)
        return 0

    lax.fori_loop(0, rows // 128, final_block, 0)

    def weight_block(j, _):
        c = pl.ds(pl.multiple_of(j * wrows, wrows), wrows)
        dw_send[j] = tn(att_full[:, c], cot_ref[...]).astype(BF16)
        return 0

    lax.fori_loop(0, ny, weight_block, 0)
    dy_copies = [
        remote(dw_send.at[ypeer(d)], dw_recv.at[y], dy_s.at[d], dy_r.at[d], ydev(ypeer(d)))
        for d in range(1, ny)
    ]
    back(2, gk_ref)
    dw_recv[y] = dw_send[y]
    for copy in dy_copies:
        copy.wait_recv()
    part = wrows // npeer

    def sum_y(j, _):
        r = pl.ds(pl.multiple_of(j * part, part), part)
        acc = dw_recv[0, r, :].astype(F32)
        for i in range(1, ny):
            acc = acc + dw_recv[i, r, :].astype(F32)
        r1_send[j] = acc.astype(BF16)
        return 0

    lax.fori_loop(0, npeer, sum_y, 0)
    dp_copies = [
        remote(r1_send.at[ppeer(d)], r1_recv.at[p], dp_s.at[d], dp_r.at[d], pdev(ppeer(d)))
        for d in range(1, npeer)
    ]
    back(3, gv_ref)
    r1_recv[p] = r1_send[p]
    for copy in dp_copies:
        copy.wait_recv()
    acc = r1_recv[0].astype(F32)
    for i in range(1, npeer):
        acc = acc + r1_recv[i].astype(F32)
    for i in range(nz):
        r2_send[i] = acc[:, i * HEAD : (i + 1) * HEAD].astype(BF16)
    dz_copies = [
        remote(r2_send.at[zpeer(d)], r2_recv.at[z], dz_s.at[d], dz_r.at[d], zdev(zpeer(d)))
        for d in range(1, nz)
    ]
    r2_recv[z] = r2_send[z]
    for copy in dz_copies:
        copy.wait_recv()
    acc = r2_recv[0].astype(F32)
    for i in range(1, nz):
        acc = acc + r2_recv[i].astype(F32)
    gz[z] = acc.astype(BF16)
    az_copies = [
        remote(gz.at[z], gz.at[z], az_s.at[d], az_r.at[d], zdev(zpeer(d))) for d in range(1, nz)
    ]
    for copy in az_copies:
        copy.wait_recv()
    gp[p] = jnp.concatenate([gz[i] for i in range(nz)], axis=1)
    ap_copies = [
        remote(gp.at[p], gp.at[p], ap_s.at[d], ap_r.at[d], pdev(ppeer(d)))
        for d in range(1, npeer)
    ]
    for copy in ap_copies:
        copy.wait_recv()
    gw_ref[...] = gp[...].reshape(wrows, gw_ref.shape[1]).astype(F32)

    for u, dst in ((1, gq_ref), (2, gk_ref), (3, gv_ref)):
        back_wait(u, dst)
    for u in range(4):
        for d in range(1, nz):
            block_wait(zbuf.at[u, zpeer(d)], zo_s.at[u, d])
        for copy in xo_copies[u]:
            copy.wait_send()
    for copies in (
        meta_copies, w_copies, t_copies, sa_copies, sb_copies,
        dy_copies, dp_copies, dz_copies, az_copies, ap_copies,
    ):
        for copy in copies:
            copy.wait_send()


def slot_tables(hist_len, token_owner, token_row, nz, npeer):
    rows = token_owner.shape[0]
    owners = nz * npeer
    match = token_owner[:, None] == jnp.arange(owners, dtype=jnp.int32)[None, :]
    before = jnp.arange(rows)[:, None] > jnp.arange(rows)[None, :]
    earlier = jnp.dot(before.astype(BF16), match.astype(BF16), preferred_element_type=F32)
    rank = jnp.sum(jnp.where(match, earlier, 0.0), axis=1).astype(jnp.int32)
    slot = lax.rem(token_owner, npeer) * (nz * SLOTS) + (token_owner // npeer) * SLOTS + rank
    at = slot[:, None] == jnp.arange(owners * SLOTS, dtype=jnp.int32)[None, :]
    row_of = jnp.min(jnp.where(at, token_row[:, None], rows), axis=0).reshape(npeer, nz * SLOTS)
    spread = jnp.broadcast_to(slot[None, :], (8, rows))
    lengths = jnp.broadcast_to(jnp.pad(hist_len, ((0, 0), (0, 120))), (8, 128))
    return jnp.concatenate([spread, row_of, lengths], axis=1)


def body(nz, npeer, ny, queries, keys, values, gates, cotangent, hist_len, token_owner, token_row, w_out):
    rows, width = queries.shape
    meta = slot_tables(hist_len, token_owner, token_row, nz, npeer)
    slots = nz * npeer * SLOTS
    wrows = w_out.shape[0]
    part = wrows // npeer
    dma = pltpu.SemaphoreType.DMA
    vmem = pl.BlockSpec(memory_space=pltpu.VMEM)
    anywhere = pl.BlockSpec(memory_space=pl.ANY)
    wide = jax.ShapeDtypeStruct((rows, width), BF16)
    out = pl.pallas_call(
        functools.partial(kernel, nz, npeer, ny),
        out_shape=(
            wide, wide, wide, wide, wide,
            jax.ShapeDtypeStruct((wrows, width), F32),
            jax.ShapeDtypeStruct((4, npeer, nz, nz, SLOTS, HEAD), BF16),
        ),
        in_specs=[anywhere, anywhere, anywhere, vmem, vmem, vmem, anywhere],
        out_specs=(vmem, anywhere, anywhere, anywhere, vmem, vmem, anywhere),
        scratch_shapes=[
            pltpu.VMEM((nz, slots, rows), BF16),
            pltpu.VMEM((nz, rows, slots), BF16),
            pltpu.VMEM((4, nz, rows, HEAD), BF16),
            pltpu.VMEM((4, npeer, nz, nz, SLOTS, HEAD), BF16),
            pltpu.VMEM((4, npeer, nz, nz, SLOTS, HEAD), BF16),
            pltpu.VMEM((4, nz, rows, HEAD), BF16),
            pltpu.VMEM((nz, rows, HEAD), BF16),
            pltpu.VMEM((ny, wrows, width), BF16),
            pltpu.VMEM((rows, width), BF16),
            pltpu.VMEM((nz, 8, META), jnp.int32),
            pltpu.VMEM((npeer, nz, 128), jnp.int32),
            pltpu.VMEM((npeer, nz, 128), jnp.int32),
            pltpu.VMEM((nz, 8, rows), F32),
            pltpu.VMEM((nz, 8, rows), F32),
            pltpu.VMEM((nz, 8, rows), F32),
            pltpu.VMEM((ny, wrows, width), BF16),
            pltpu.VMEM((ny, wrows, width), BF16),
            pltpu.VMEM((npeer, part, width), BF16),
            pltpu.VMEM((npeer, part, width), BF16),
            pltpu.VMEM((nz, part, HEAD), BF16),
            pltpu.VMEM((nz, part, HEAD), BF16),
            pltpu.VMEM((nz, part, HEAD), BF16),
            pltpu.VMEM((npeer, part, width), BF16),
            dma((5,)),
            dma((4, nz)), dma((4, nz)),
            dma((4, npeer)), dma((4, npeer)),
            dma((4, npeer)), dma((4, npeer)),
            dma((4, nz)), dma((4, nz)),
            dma((nz,)), dma((nz,)),
            dma((npeer,)), dma((npeer,)),
            dma((ny,)), dma((ny,)),
            dma((nz,)), dma((nz,)),
            dma((nz,)), dma((nz,)),
            dma((ny,)), dma((ny,)),
            dma((npeer,)), dma((npeer,)),
            dma((nz,)), dma((nz,)),
            dma((nz,)), dma((nz,)),
            dma((npeer,)), dma((npeer,)),
        ],
        compiler_params=pltpu.CompilerParams(
            collective_id=0, has_side_effects=True, vmem_limit_bytes=63 * 1024 * 1024
        ),
    )(queries, keys, values, gates, cotangent, meta, w_out)
    return out[:6]


def solution(mesh):
    ny = mesh.shape["dp"]
    nz = 8
    npeer = mesh.shape["bal"] // nz
    token = P(("dp", "bal"))
    wide = P(("dp", "bal"), None)
    return jax.shard_map(
        functools.partial(body, nz, npeer, ny),
        mesh=mesh,
        in_specs=(wide, wide, wide, wide, wide, wide, token, token, P("dp", None)),
        out_specs=(wide, wide, wide, wide, wide, P("dp", None)),
        check_vma=False,
    )
```

```python
import functools
import math

import jax
import jax.numpy as jnp
from jax import lax
from jax.experimental import pallas as pl
from jax.experimental.pallas import tpu as pltpu
from jax.sharding import PartitionSpec as P

HEAD = 128
EPSILON = 1e-05
SLOTS = 16
MESH = pl.DeviceIdType.MESH
F32 = jnp.float32
BF16 = jnp.bfloat16
META = 768


def nn(a, b):
    return lax.dot_general(a, b, (((1,), (0,)), ((), ())), preferred_element_type=F32)


def nt(a, b):
    return lax.dot_general(a, b, (((1,), (1,)), ((), ())), preferred_element_type=F32)


def tn(a, b):
    return lax.dot_general(a, b, (((0,), (0,)), ((), ())), preferred_element_type=F32)


def block_wait(ref, sem):
    pltpu.make_async_copy(ref, ref, sem).wait()


def kernel(
    nz, npeer, ny,
    q_ref, k_ref, v_ref, gates_ref, cot_ref, owner_ref, row_ref, len_ref, w_ref,
    out_to, gq_ref, gk_ref, gv_ref, gg_to, gw_ref,
    out_ref, gg_ref, onehot_src, onehot_own, zbuf, xsend, xrecv, own, att_own, wbuf, wfull, att_full,
    metaz, hist, tsend, trecv, stat_s, stat_r, stat_f,
    pair_recv, dw_recv, r1_send, r1_recv, r2_send, r2_recv, gz,
    loc, zin_s, zin_r, xin_s, xin_r, xo_s, xo_r, zo_s, zo_r,
    m_s, m_r, t_s, t_r, w_s, w_r, sa_s, sa_r, sb_s, sb_r,
    pr_s, pr_r, dy_s, dy_r, dp_s, dp_r, dz_s, dz_r, az_s, az_r, ap_s, ap_r,
):
    y = lax.axis_index("dp")
    b = lax.axis_index("bal")
    z = b // npeer
    p = lax.rem(b, npeer)
    rows = q_ref.shape[0]
    wrows = wfull.shape[1]
    part = wrows // npeer
    half = rows // 2
    slots = npeer * nz * SLOTS
    scale = 1.0 / math.sqrt(HEAD)
    order = [0]
    for d in range(1, nz // 2 + 1):
        order += [d, nz - d] if 2 * d < nz else [d]
    chunks = 4
    per = nz // chunks
    bounds = (0, 1, 2, 4, 6, 8)

    def zpeer(d):
        return lax.rem(z + d, nz)

    def ppeer(d):
        return lax.rem(p + d, npeer)

    def ypeer(d):
        return lax.rem(y + d, ny)

    def zdev(at):
        return (y, at * npeer + p)

    def pdev(at):
        return (y, z * npeer + at)

    def ydev(at):
        return (at, b)

    def columns(at):
        return pl.ds(pl.multiple_of(at * HEAD, HEAD), HEAD)

    def remote(src, dst, ssem, rsem, device):
        copy = pltpu.make_async_remote_copy(
            src_ref=src, dst_ref=dst, send_sem=ssem, recv_sem=rsem,
            device_id=device, device_id_type=MESH,
        )
        copy.start()
        return copy

    barrier = pltpu.get_barrier_semaphore()
    for d in range(1, nz):
        pl.semaphore_signal(barrier, inc=1, device_id=zdev(zpeer(d)), device_id_type=MESH)
    for d in range(1, npeer):
        pl.semaphore_signal(barrier, inc=1, device_id=pdev(ppeer(d)), device_id_type=MESH)
    for d in range(1, ny):
        pl.semaphore_signal(barrier, inc=1, device_id=ydev(ypeer(d)), device_id_type=MESH)

    owner = owner_ref[...]
    column = jnp.broadcast_to(owner.astype(F32), (128, rows)).T[:, 0:1]
    first = lax.broadcasted_iota(jnp.int32, (rows, rows), 0)
    second = lax.broadcasted_iota(jnp.int32, (rows, rows), 1)
    same = (column == owner.astype(F32)) & (first < second)
    rank = jnp.sum(jnp.where(same, 1.0, 0.0), axis=0, keepdims=True).astype(jnp.int32)
    slot = lax.rem(owner, npeer) * (nz * SLOTS) + lax.div(owner, npeer) * SLOTS + rank
    metaz[0, :, 0:rows] = jnp.broadcast_to(slot, (8, rows))

    def build_src(i, _):
        slot = metaz[i, 0:1, 0:rows]
        for c in range(slots // 128):
            ids = lax.broadcasted_iota(jnp.int32, (128, rows), 0) + c * 128
            onehot_src[i, c * 128 : (c + 1) * 128, :] = jnp.where(ids == slot, 1.0, 0.0).astype(BF16)
        return 0

    build_src(0, 0)
    token_row = jnp.broadcast_to(row_ref[...], (8, rows))
    line = lax.broadcasted_iota(jnp.int32, (8, rows), 0)
    digits = jnp.where(
        line == 0, lax.div(token_row, 16), jnp.where(line == 1, lax.rem(token_row, 16), 1)
    )
    found = nt(digits.astype(F32).astype(BF16), onehot_src[0])
    row_of = found[0:1] * 16.0 + found[1:2] + (1.0 - found[2:3]) * rows
    row_of = row_of.astype(jnp.int32)
    metaz[0, :, 512:640] = jnp.concatenate(
        [row_of[:, i * nz * SLOTS : (i + 1) * nz * SLOTS] for i in range(npeer)], axis=0
    )
    metaz[0, :, 640:768] = jnp.broadcast_to(len_ref[...], (8, 128))

    pl.semaphore_wait(barrier, nz + npeer + ny - 3)

    meta_copies = [
        remote(metaz.at[0], metaz.at[j], m_s.at[j], m_r.at[j], zdev(zpeer(order[j])))
        for j in range(1, nz)
    ]
    def z_in(u, src):
        pltpu.make_async_copy(src.at[:, columns(z)], zbuf.at[u, 0], zin_r.at[u, 0]).start()
        for j in range(1, nz):
            to = zpeer(order[j])
            remote(src.at[:, columns(to)], zbuf.at[u, j], zin_s.at[u], zin_r.at[u, j], zdev(to))

    z_in(0, q_ref)
    w_copies = [
        remote(w_ref, wfull.at[y], w_s.at[d], w_r.at[d], ydev(ypeer(d))) for d in range(1, ny)
    ]
    w_local = pltpu.make_async_copy(w_ref, wfull.at[y], loc.at[0])
    w_local.start()
    z_in(1, k_ref)
    z_in(2, v_ref)
    def pack_in(u, i):
        lo, hi = bounds[i], bounds[i + 1]
        places = slice(lo, hi)

        def step(j, _):
            block_wait(zbuf.at[u, j], zin_r.at[u, j])
            moved = nn(onehot_src[j], zbuf[u, j]).astype(BF16)
            xsend[u, :, :, j] = moved.reshape(npeer, nz, SLOTS, HEAD)
            return 0

        lax.fori_loop(lo, hi, step, 0)
        for d in range(1, npeer):
            to = ppeer(d)
            remote(
                xsend.at[u, to, :, places], xrecv.at[u, p, :, places], xin_s.at[u], xin_r.at[u],
                pdev(to),
            )
        if hi == nz:
            pltpu.make_async_copy(xsend.at[u, p], xrecv.at[u, p], xin_r.at[u]).start()

    def unpack_in(u):
        block_wait(xrecv.at[u], xin_r.at[u])

        def step(o, _):
            own[u, o] = nn(onehot_own[o], xrecv[u, :, o].reshape(slots, HEAD)).astype(BF16)
            return 0

        lax.fori_loop(0, nz, step, 0)

    for u in range(3):
        pack_in(u, 0)

    for copy in meta_copies:
        copy.wait_recv()
    for j in range(nz):
        hist[zpeer(nz - order[j])] = metaz[j, :, 640:768]
    for at in range(npeer):
        tsend[at] = metaz[:, at, 512:640]
    t_copies = [
        remote(tsend.at[ppeer(d)], trecv.at[p], t_s.at[d], t_r.at[d], pdev(ppeer(d)))
        for d in range(1, npeer)
    ]
    trecv[p] = tsend[p]
    lax.fori_loop(1, nz, build_src, 0)

    pack_in(0, 1)

    for copy in t_copies:
        copy.wait_recv()
    group = npeer * nz

    def build_own(o, _):
        table = trecv[...].reshape(group, 128)
        high = (table // 16).astype(F32).astype(BF16)
        low = (table % 16).astype(F32).astype(BF16)
        lane = lax.broadcasted_iota(jnp.int32, (128, slots), 1)
        take = lax.broadcasted_iota(jnp.int32, (128, slots), 0)
        pick = jnp.where(take == o * SLOTS + lane % SLOTS, 1.0, 0.0).astype(BF16)
        spread = nn(high, pick) * 16.0 + nn(low, pick)
        which = lax.broadcasted_iota(jnp.int32, (group, slots), 0)
        at = lax.broadcasted_iota(jnp.int32, (group, slots), 1) // SLOTS
        row = jnp.sum(jnp.where(which == at, spread, 0.0), axis=0, keepdims=True).astype(jnp.int32)
        for c in range(rows // 128):
            ids = lax.broadcasted_iota(jnp.int32, (128, slots), 0) + c * 128
            onehot_own[o, c * 128 : (c + 1) * 128, :] = jnp.where(ids == row, 1.0, 0.0).astype(BF16)
        return 0

    lax.fori_loop(0, nz, build_own, 0)

    def allowed_of(o):
        lengths = hist[o, 0:1, :]
        line = lax.broadcasted_iota(jnp.int32, (rows, 1), 0)
        end = jnp.zeros((1, 1), jnp.int32)
        start = jnp.zeros((rows, 1), jnp.int32)
        for h in range(8):
            length = lengths[:, h : h + 1]
            end = end + length
            start = start + jnp.where(line >= end, length, 0)
        i = lax.broadcasted_iota(jnp.int32, (rows, rows), 0)
        j = lax.broadcasted_iota(jnp.int32, (rows, rows), 1)
        return (j <= i) & (j >= start)

    def weigh(o, _):
        scores = nt(own[0, o], own[1, o]) * scale
        sig = 0.5 * jnp.tanh(0.5 * scores) + 0.5
        weights = jnp.where(allowed_of(o), scores * sig, 0.0).astype(BF16)
        wbuf[o, :, 0:rows] = weights[0:half]
        wbuf[o, :, rows:] = weights[half:]
        return 0

    def weights_of(o):
        return jnp.concatenate([wbuf[o, :, 0:rows], wbuf[o, :, rows:]], axis=0)

    def attend(o, _):
        att = nn(weights_of(o), own[2, o]).astype(BF16)
        att_own[o] = att
        moved = tn(att, onehot_own[o]).astype(BF16).T
        xsend[0, :, o] = moved.reshape(npeer, nz, SLOTS, HEAD)
        return 0

    def sent_in(u):
        block_wait(xsend.at[u, 1:npeer], xin_s.at[u])

    for i in range(2, 5):
        pack_in(0, i)
    pack_in(1, 1)
    pack_in(1, 2)

    w_local.wait()
    for copy in w_copies:
        copy.wait_recv()

    def dz_block(i, _):
        r = pl.ds(pl.multiple_of(i * 128, 128), 128)
        cot = cot_ref[r, :]
        for j in range(ny):
            c = slice(j * wrows, (j + 1) * wrows)
            gg_ref[r, c] = (nt(cot, wfull[j]) * gates_ref[r, c].astype(F32)).astype(BF16)
        return 0

    lax.fori_loop(0, rows // 128, dz_block, 0)
    z_in(3, gg_ref)

    unpack_in(0)
    pack_in(1, 3)
    pack_in(1, 4)
    pack_in(3, 0)
    pack_in(2, 1)
    pack_in(2, 2)
    unpack_in(1)
    pack_in(2, 3)
    lax.fori_loop(0, nz // 2, weigh, 0)
    pack_in(2, 4)
    lax.fori_loop(nz // 2, nz, weigh, 0)
    pack_in(3, 1)
    pack_in(3, 2)
    unpack_in(2)
    pack_in(3, 3)
    sent_in(0)
    lax.fori_loop(0, nz // 2, attend, 0)
    pack_in(3, 4)
    lax.fori_loop(nz // 2, nz, attend, 0)

    into = (0, 1, 2, 4)

    def x_out(u, parts=(3, 2, 1, 0), owners=slice(0, nz)):
        for i in parts:
            places = slice(i * per, (i + 1) * per)
            for d in range(1, npeer):
                to = ppeer(d)
                remote(
                    xsend.at[u, to, owners, places], xrecv.at[into[u], p, owners, places],
                    xo_s.at[u], xo_r.at[u, i], pdev(to),
                )
            pltpu.make_async_copy(
                xsend.at[u, p, owners, places], xrecv.at[into[u], p, owners, places],
                xo_r.at[u, i],
            ).start()

    def back(u, dst, i):
        places = slice(i * per, (i + 1) * per)
        block_wait(xrecv.at[into[u], :, :, places], xo_r.at[u, i])

        def tokens(j, _):
            got = xrecv[into[u], :, :, j].reshape(slots, HEAD)
            zbuf[u, j] = tn(got, onehot_src[j]).astype(BF16).T
            return 0

        lax.fori_loop(i * per, (i + 1) * per, tokens, 0)
        for j in range(i * per, (i + 1) * per):
            if j == 0:
                pltpu.make_async_copy(zbuf.at[u, 0], dst.at[:, columns(z)], zo_r.at[u]).start()
            else:
                remote(
                    zbuf.at[u, j], dst.at[:, columns(z)], zo_s.at[u], zo_r.at[u],
                    zdev(zpeer(nz - order[j])),
                )

    x_out(0, (0, 1, 3, 2))

    block_wait(xrecv.at[3], xin_r.at[3])

    def stats(o, _):
        moved = nn(onehot_own[o], xrecv[3, :, o].reshape(slots, HEAD)).astype(BF16)
        own[3, o] = moved
        att = att_own[o].astype(F32)
        dz = moved.astype(F32)
        mean = jnp.sum(att, axis=1, keepdims=True) * (1.0 / HEAD)
        cent = att - mean
        second = jnp.sum(cent * cent, axis=1, keepdims=True)
        total = jnp.sum(dz, axis=1, keepdims=True)
        cross = jnp.sum(dz * cent, axis=1, keepdims=True)
        lane = lax.broadcasted_iota(jnp.int32, (rows, HEAD), 1)
        table = jnp.where(
            lane == 0, mean, jnp.where(lane == 1, second, jnp.where(lane == 2, total, cross))
        )
        stat_s[o] = table.T[0:8, :]
        return 0

    lax.fori_loop(0, nz, stats, 0)
    sa_copies = [
        remote(stat_s.at[zpeer(d)], stat_r.at[z], sa_s.at[d], sa_r.at[d], zdev(zpeer(d)))
        for d in range(1, nz)
    ]
    stat_r[z] = stat_s[z]
    back(0, att_full, 0)
    for copy in sa_copies:
        copy.wait_recv()
    features = float(nz * HEAD)
    got = stat_r[...]
    means, seconds, totals, crosses = [got[:, i : i + 1, :] for i in range(4)]
    mean = jnp.sum(means, axis=0) * (1.0 / nz)
    shift = means - mean[None]
    var = (jnp.sum(seconds, axis=0) + HEAD * jnp.sum(shift * shift, axis=0)) / features
    inverse = lax.rsqrt(var + EPSILON)
    mean_grad = jnp.sum(totals, axis=0) / features
    mean_cross = jnp.sum(crosses + shift * totals, axis=0) * inverse / features
    stat_f[z] = jnp.concatenate([mean, inverse, mean_grad, mean_cross] * 2, axis=0)
    sb_copies = [
        remote(stat_f.at[z], stat_f.at[z], sb_s.at[d], sb_r.at[d], zdev(zpeer(d)))
        for d in range(1, nz)
    ]
    back(0, att_full, 1)
    for u in range(1, 4):
        sent_in(u)
    for copy in sb_copies:
        copy.wait_recv()

    def value_grads(o, _):
        full = jnp.concatenate([stat_f[o]] * (HEAD // 8), axis=0).T
        mean, inverse = full[:, 0:1], full[:, 1:2]
        mean_grad, mean_cross = full[:, 2:3], full[:, 3:4]
        normed = (att_own[o].astype(F32) - mean) * inverse
        grad = (own[3, o].astype(F32) - mean_grad - normed * mean_cross) * inverse
        grad = grad.astype(BF16)
        own[3, o] = grad
        gv_t = tn(grad, weights_of(o)).astype(BF16)
        xsend[1, :, o] = nn(gv_t, onehot_own[o]).astype(BF16).T.reshape(npeer, nz, SLOTS, HEAD)
        return 0

    def score_grads(o, _):
        q, k, v, grad = own[0, o], own[1, o], own[2, o], own[3, o]
        scores = nt(q, k) * scale
        sig = 0.5 * jnp.tanh(0.5 * scores) + 0.5
        slope = sig + scores * sig * (1.0 - sig)
        gs = jnp.where(allowed_of(o), nt(grad, v) * slope * scale, 0.0).astype(BF16)
        gq_t = nn(gs, k).astype(BF16)
        gk_t = tn(q, gs).astype(BF16)
        spots = onehot_own[o]
        xsend[2, :, o] = tn(gq_t, spots).astype(BF16).T.reshape(npeer, nz, SLOTS, HEAD)
        xsend[3, :, o] = nn(gk_t, spots).astype(BF16).T.reshape(npeer, nz, SLOTS, HEAD)
        return 0

    back(0, att_full, 3)
    lax.fori_loop(0, nz, value_grads, 0)
    x_out(1)
    back(0, att_full, 2)
    lax.fori_loop(0, 4, score_grads, 0)
    for u in range(4):
        block_wait(zbuf.at[u, 1:nz], zin_s.at[u])
    back(1, gv_ref, 3)
    lax.fori_loop(4, 6, score_grads, 0)
    back(1, gv_ref, 2)

    block_wait(att_full, zo_r.at[0])

    def final_block(i, _):
        r = pl.ds(pl.multiple_of(i * 128, 128), 128)
        att = att_full[r, :].astype(F32)
        cent = att - jnp.mean(att, axis=1, keepdims=True)
        inv = lax.rsqrt(jnp.mean(cent * cent, axis=1, keepdims=True) + EPSILON)
        normed = cent * inv
        gated = (normed * gates_ref[r, :].astype(F32)).astype(BF16)
        att_full[r, :] = gated
        cot = cot_ref[r, :]
        acc = None
        for j in range(ny):
            c = slice(j * wrows, (j + 1) * wrows)
            gg_ref[r, c] = (nt(cot, wfull[j]) * normed[:, c]).astype(BF16)
            step = nn(gated[:, c], wfull[j])
            acc = step if acc is None else acc + step
        out_ref[r, :] = acc.astype(BF16)
        return 0

    lax.fori_loop(0, rows // 128, final_block, 0)
    out_copy = pltpu.make_async_copy(out_ref, out_to, loc.at[1])
    out_copy.start()
    gg_copy = pltpu.make_async_copy(gg_ref, gg_to, loc.at[2])
    gg_copy.start()

    def weight_block(j, _):
        c = pl.ds(pl.multiple_of(j * wrows, wrows), wrows)
        wbuf[j] = tn(att_full[:, c], cot_ref[...]).astype(BF16)
        return 0

    lax.fori_loop(0, ny, weight_block, 0)
    core = lax.rem(p, 2)
    chip = lax.div(p, 2)
    chips = npeer // 2
    mine = pl.ds(pl.multiple_of(core * (wrows // 2), wrows // 2), wrows // 2)
    theirs = pl.ds(pl.multiple_of((1 - core) * (wrows // 2), wrows // 2), wrows // 2)
    pair = remote(
        wbuf.at[0:ny, theirs], pair_recv, pr_s.at[0], pr_r.at[0], pdev(chip * 2 + 1 - core)
    )
    lax.fori_loop(6, nz, score_grads, 0)
    x_out(2, (3, 2, 1))
    back(1, gv_ref, 1)
    pair.wait_recv()

    def sum_pair(j, _):
        wbuf[j, mine] = (wbuf[j, mine].astype(F32) + pair_recv[j].astype(F32)).astype(BF16)
        return 0

    lax.fori_loop(0, ny, sum_pair, 0)
    dy_copies = [
        remote(wbuf.at[ypeer(d), mine], dw_recv.at[y], dy_s.at[d], dy_r.at[d], ydev(ypeer(d)))
        for d in range(1, ny)
    ]
    dw_recv[y] = wbuf[y, mine]
    back(1, gv_ref, 0)
    back(2, gq_ref, 3)

    for copy in dy_copies:
        copy.wait_recv()

    def sum_y(j, _):
        r = pl.ds(pl.multiple_of(j * part, part), part)
        acc = dw_recv[0, r, :].astype(F32)
        for i in range(1, ny):
            acc = acc + dw_recv[i, r, :].astype(F32)
        r1_send[j] = acc.astype(BF16)
        return 0

    lax.fori_loop(0, chips, sum_y, 0)
    dp_copies = []
    for d in range(1, chips):
        to = lax.rem(chip + d, chips)
        dp_copies.append(
            remote(
                r1_send.at[to], r1_recv.at[chip], dp_s.at[d], dp_r.at[d], pdev(to * 2 + core)
            )
        )
    r1_recv[chip] = r1_send[chip]
    x_out(2, (0,))
    back(2, gq_ref, 2)
    for copy in dp_copies:
        copy.wait_recv()
    acc = r1_recv[0].astype(F32)
    for i in range(1, chips):
        acc = acc + r1_recv[i].astype(F32)
    for i in range(nz):
        r2_send[i] = acc[:, i * HEAD : (i + 1) * HEAD].astype(BF16)
    dz_copies = [
        remote(r2_send.at[zpeer(d)], r2_recv.at[z], dz_s.at[d], dz_r.at[d], zdev(zpeer(d)))
        for d in range(1, nz)
    ]
    r2_recv[z] = r2_send[z]
    x_out(3, (3, 2))
    back(2, gq_ref, 1)
    back(2, gq_ref, 0)
    for copy in dz_copies:
        copy.wait_recv()
    acc = r2_recv[0].astype(F32)
    for i in range(1, nz):
        acc = acc + r2_recv[i].astype(F32)
    gz[z] = acc.astype(BF16)
    az_copies = [
        remote(gz.at[z], gz.at[z], az_s.at[d], az_r.at[d], zdev(zpeer(d))) for d in range(1, nz)
    ]
    x_out(3, (1, 0))
    back(3, gk_ref, 3)
    back(3, gk_ref, 2)
    for copy in az_copies:
        copy.wait_recv()
    place = core * chips + chip
    gw_ref[place] = jnp.concatenate([gz[i] for i in range(nz)], axis=1)
    ap_copies = [
        remote(gw_ref.at[place], gw_ref.at[place], ap_s.at[d], ap_r.at[d], pdev(ppeer(d)))
        for d in range(1, npeer)
    ]
    back(3, gk_ref, 1)
    back(3, gk_ref, 0)
    for copy in ap_copies:
        copy.wait_recv()

    out_copy.wait()
    gg_copy.wait()
    for u, dst in ((1, gv_ref), (2, gq_ref), (3, gk_ref)):
        block_wait(dst, zo_r.at[u])
    for u in range(4):
        block_wait(zbuf.at[u, 1:nz], zo_s.at[u])
        block_wait(xsend.at[u, 1:npeer], xo_s.at[u])
    for copies in (
        meta_copies, w_copies, t_copies, sa_copies, sb_copies,
        [pair], dy_copies, dp_copies, dz_copies, az_copies, ap_copies,
    ):
        for copy in copies:
            copy.wait_send()


def settle(*refs):
    for src, dst in zip(refs[:5], refs[6:11]):
        dst[...] = src[...]
    refs[11][...] = refs[5][...].reshape(refs[11].shape).astype(F32)


def body(nz, npeer, ny, queries, keys, values, gates, cotangent, hist_len, token_owner, token_row, w_out):
    rows, width = queries.shape
    lengths = jnp.pad(hist_len, ((0, 0), (0, 120)))
    slots = nz * npeer * SLOTS
    wrows = w_out.shape[0]
    part = wrows // npeer
    dma = pltpu.SemaphoreType.DMA
    vmem = pl.BlockSpec(memory_space=pltpu.VMEM)
    anywhere = pl.BlockSpec(memory_space=pl.ANY)
    wide = jax.ShapeDtypeStruct((rows, width), BF16)
    out = pl.pallas_call(
        functools.partial(kernel, nz, npeer, ny),
        out_shape=(
            wide, wide, wide, wide, wide,
            jax.ShapeDtypeStruct((npeer, part, width), BF16),
        ),
        in_specs=[anywhere, anywhere, anywhere, vmem, vmem, vmem, vmem, vmem, anywhere],
        out_specs=(anywhere, anywhere, anywhere, anywhere, anywhere, vmem),
        scratch_shapes=[
            pltpu.VMEM((rows, width), BF16),
            pltpu.VMEM((rows, width), BF16),
            pltpu.VMEM((nz, slots, rows), BF16),
            pltpu.VMEM((nz, rows, slots), BF16),
            pltpu.VMEM((4, nz, rows, HEAD), BF16),
            pltpu.VMEM((4, npeer, nz, nz, SLOTS, HEAD), BF16),
            pltpu.VMEM((5, npeer, nz, nz, SLOTS, HEAD), BF16),
            pltpu.VMEM((4, nz, rows, HEAD), BF16),
            pltpu.VMEM((nz, rows, HEAD), BF16),
            pltpu.VMEM((nz, rows // 2, 2 * rows), BF16),
            pltpu.VMEM((ny, wrows, width), BF16),
            pltpu.VMEM((rows, width), BF16),
            pltpu.VMEM((nz, 8, META), jnp.int32),
            pltpu.VMEM((nz, 8, 128), jnp.int32),
            pltpu.VMEM((npeer, nz, 128), jnp.int32),
            pltpu.VMEM((npeer, nz, 128), jnp.int32),
            pltpu.VMEM((nz, 8, rows), F32),
            pltpu.VMEM((nz, 8, rows), F32),
            pltpu.VMEM((nz, 8, rows), F32),
            pltpu.VMEM((ny, wrows // 2, width), BF16),
            pltpu.VMEM((ny, wrows // 2, width), BF16),
            pltpu.VMEM((npeer // 2, part, width), BF16),
            pltpu.VMEM((npeer // 2, part, width), BF16),
            pltpu.VMEM((nz, part, HEAD), BF16),
            pltpu.VMEM((nz, part, HEAD), BF16),
            pltpu.VMEM((nz, part, HEAD), BF16),
            dma((3,)),
            dma((4,)), dma((4, nz)),
            dma((4,)), dma((4,)),
            dma((4,)), dma((4, 4)),
            dma((4,)), dma((4,)),
            dma((nz,)), dma((nz,)),
            dma((npeer,)), dma((npeer,)),
            dma((ny,)), dma((ny,)),
            dma((nz,)), dma((nz,)),
            dma((nz,)), dma((nz,)),
            dma((1,)), dma((1,)),
            dma((ny,)), dma((ny,)),
            dma((npeer // 2,)), dma((npeer // 2,)),
            dma((nz,)), dma((nz,)),
            dma((nz,)), dma((nz,)),
            dma((npeer,)), dma((npeer,)),
        ],
        compiler_params=pltpu.CompilerParams(
            collective_id=0, has_side_effects=True, vmem_limit_bytes=63 * 1024 * 1024
        ),
    )(
        queries, keys, values, gates, cotangent,
        token_owner.reshape(1, rows), token_row.reshape(1, rows), lengths, w_out,
    )
    out, gq, gk, gv, gg, gw = out
    steps = 4
    block = pl.BlockSpec((rows // steps, width), lambda i: (i, 0))
    gq, gk, gv, out, gg, gw = pl.pallas_call(
        settle,
        grid=(steps,),
        out_shape=(wide,) * 5 + (jax.ShapeDtypeStruct((wrows, width), F32),),
        in_specs=[block] * 5 + [pl.BlockSpec((npeer // steps, part, width), lambda i: (i, 0, 0))],
        out_specs=(block,) * 5 + (pl.BlockSpec((wrows // steps, width), lambda i: (i, 0)),),
        compiler_params=pltpu.CompilerParams(vmem_limit_bytes=60 * 1024 * 1024),
    )(gq, gk, gv, out, gg, gw)
    return out, gq, gk, gv, gg, gw


def solution(mesh):
    ny = mesh.shape["dp"]
    nz = 8
    npeer = mesh.shape["bal"] // nz
    token = P(("dp", "bal"))
    wide = P(("dp", "bal"), None)
    return jax.shard_map(
        functools.partial(body, nz, npeer, ny),
        mesh=mesh,
        in_specs=(wide, wide, wide, wide, wide, wide, token, token, P("dp", None)),
        out_specs=(wide, wide, wide, wide, wide, P("dp", None)),
        check_vma=False,
    )
```

```python
import functools
import math

import jax
import jax.numpy as jnp
from jax import lax
from jax.experimental import pallas as pl
from jax.experimental.pallas import tpu as pltpu
from jax.sharding import PartitionSpec as P

HEAD = 128
EPSILON = 1e-05
SLOTS = 16
MESH = pl.DeviceIdType.MESH
F32 = jnp.float32
BF16 = jnp.bfloat16
META = 768


def nn(a, b):
    return lax.dot_general(a, b, (((1,), (0,)), ((), ())), preferred_element_type=F32)


def nt(a, b):
    return lax.dot_general(a, b, (((1,), (1,)), ((), ())), preferred_element_type=F32)


def tn(a, b):
    return lax.dot_general(a, b, (((0,), (0,)), ((), ())), preferred_element_type=F32)


def block_wait(ref, sem):
    pltpu.make_async_copy(ref, ref, sem).wait()


def kernel(
    nz, npeer, ny,
    q_ref, k_ref, v_ref, gates_ref, cot_ref, owner_ref, row_ref, len_ref, w_ref,
    out_to, gq_ref, gk_ref, gv_ref, gg_to, gw_ref,
    out_ref, gg_ref, onehot_src, onehot_own, zbuf, xsend, xrecv, own, att_own, wbuf, wfull, att_full,
    metaz, hist, tsend, trecv, stat_s, stat_r, stat_f,
    pair_recv, dw_recv, r1_send, r1_recv, r2_send, r2_recv, gz,
    loc, zin_s, zin_r, xin_s, xin_r, xo_s, xo_r, zo_s, zo_r,
    m_s, m_r, t_s, t_r, w_s, w_r, sa_s, sa_r, sb_s, sb_r,
    pr_s, pr_r, dy_s, dy_r, dp_s, dp_r, dz_s, dz_r, az_s, az_r, ap_s, ap_r,
):
    y = lax.axis_index("dp")
    b = lax.axis_index("bal")
    z = b // npeer
    p = lax.rem(b, npeer)
    rows = q_ref.shape[0]
    wrows = wfull.shape[1]
    part = wrows // npeer
    half = rows // 2
    slots = npeer * nz * SLOTS
    scale = 1.0 / math.sqrt(HEAD)
    order = [0]
    for d in range(1, nz // 2 + 1):
        order += [d, nz - d] if 2 * d < nz else [d]
    bounds = (0, 1, 3, 5, 7, 8)
    groups = ((0, 3), (3, 5), (5, 7), (7, 8))

    def zpeer(d):
        return lax.rem(z + d, nz)

    def ppeer(d):
        return lax.rem(p + d, npeer)

    def ypeer(d):
        return lax.rem(y + d, ny)

    def zdev(at):
        return (y, at * npeer + p)

    def pdev(at):
        return (y, z * npeer + at)

    def ydev(at):
        return (at, b)

    def columns(at):
        return pl.ds(pl.multiple_of(at * HEAD, HEAD), HEAD)

    def remote(src, dst, ssem, rsem, device):
        copy = pltpu.make_async_remote_copy(
            src_ref=src, dst_ref=dst, send_sem=ssem, recv_sem=rsem,
            device_id=device, device_id_type=MESH,
        )
        copy.start()
        return copy

    barrier = pltpu.get_barrier_semaphore()
    for d in range(1, nz):
        pl.semaphore_signal(barrier, inc=1, device_id=zdev(zpeer(d)), device_id_type=MESH)
    for d in range(1, npeer):
        pl.semaphore_signal(barrier, inc=1, device_id=pdev(ppeer(d)), device_id_type=MESH)
    for d in range(1, ny):
        pl.semaphore_signal(barrier, inc=1, device_id=ydev(ypeer(d)), device_id_type=MESH)

    owner = owner_ref[...]
    column = jnp.broadcast_to(owner.astype(F32), (128, rows)).T[:, 0:1]
    first = lax.broadcasted_iota(jnp.int32, (rows, rows), 0)
    second = lax.broadcasted_iota(jnp.int32, (rows, rows), 1)
    same = (column == owner.astype(F32)) & (first < second)
    rank = jnp.sum(jnp.where(same, 1.0, 0.0), axis=0, keepdims=True).astype(jnp.int32)
    slot = lax.rem(owner, npeer) * (nz * SLOTS) + lax.div(owner, npeer) * SLOTS + rank
    metaz[0, :, 0:rows] = jnp.broadcast_to(slot, (8, rows))

    def build_src(i, _):
        slot = metaz[i, 0:1, 0:rows]
        for c in range(slots // 128):
            ids = lax.broadcasted_iota(jnp.int32, (128, rows), 0) + c * 128
            onehot_src[i, c * 128 : (c + 1) * 128, :] = jnp.where(ids == slot, 1.0, 0.0).astype(BF16)
        return 0

    build_src(0, 0)
    token_row = jnp.broadcast_to(row_ref[...], (8, rows))
    line = lax.broadcasted_iota(jnp.int32, (8, rows), 0)
    digits = jnp.where(
        line == 0, lax.div(token_row, 16), jnp.where(line == 1, lax.rem(token_row, 16), 1)
    )
    found = nt(digits.astype(F32).astype(BF16), onehot_src[0])
    row_of = found[0:1] * 16.0 + found[1:2] + (1.0 - found[2:3]) * rows
    row_of = row_of.astype(jnp.int32)
    metaz[0, :, 512:640] = jnp.concatenate(
        [row_of[:, i * nz * SLOTS : (i + 1) * nz * SLOTS] for i in range(npeer)], axis=0
    )
    metaz[0, :, 640:648] = jnp.broadcast_to(len_ref[...], (8, 8))

    pl.semaphore_wait(barrier, nz + npeer + ny - 3)

    meta_copies = [
        remote(metaz.at[0], metaz.at[j], m_s.at[j], m_r.at[j], zdev(zpeer(order[j])))
        for j in range(1, nz)
    ]
    def z_in(u, src):
        pltpu.make_async_copy(src.at[:, columns(z)], zbuf.at[u, 0], zin_r.at[u, 0]).start()
        for j in range(1, nz):
            to = zpeer(order[j])
            remote(src.at[:, columns(to)], zbuf.at[u, j], zin_s.at[u], zin_r.at[u, j], zdev(to))

    z_in(0, q_ref)
    w_copies = [
        remote(w_ref, wfull.at[y], w_s.at[d], w_r.at[d], ydev(ypeer(d))) for d in range(1, ny)
    ]
    w_local = pltpu.make_async_copy(w_ref, wfull.at[y], loc.at[0])
    w_local.start()
    z_in(1, k_ref)
    z_in(2, v_ref)
    def pack_in(u, i):
        lo, hi = bounds[i], bounds[i + 1]
        places = slice(lo, hi)

        def step(j, _):
            block_wait(zbuf.at[u, j], zin_r.at[u, j])
            moved = nn(onehot_src[j], zbuf[u, j]).astype(BF16)
            xsend[u, :, :, j] = moved.reshape(npeer, nz, SLOTS, HEAD)
            return 0

        lax.fori_loop(lo, hi, step, 0)
        for d in range(1, npeer):
            to = ppeer(d)
            remote(
                xsend.at[u, to, :, places], xrecv.at[u, p, :, places], xin_s.at[u], xin_r.at[u],
                pdev(to),
            )
        if hi == nz:
            pltpu.make_async_copy(xsend.at[u, p], xrecv.at[u, p], xin_r.at[u]).start()

    def unpack_in(u):
        block_wait(xrecv.at[u], xin_r.at[u])

        def step(o, _):
            own[u, o] = nn(onehot_own[o], xrecv[u, :, o].reshape(slots, HEAD)).astype(BF16)
            return 0

        lax.fori_loop(0, nz, step, 0)

    for u in range(3):
        pack_in(u, 0)

    for copy in meta_copies:
        copy.wait_recv()
    for j in range(nz):
        hist[zpeer(nz - order[j])] = metaz[j, :, 640:768]
    for at in range(npeer):
        tsend[at] = metaz[:, at, 512:640]
    t_copies = [
        remote(tsend.at[ppeer(d)], trecv.at[p], t_s.at[d], t_r.at[d], pdev(ppeer(d)))
        for d in range(1, npeer)
    ]
    trecv[p] = tsend[p]
    lax.fori_loop(1, nz, build_src, 0)

    pack_in(0, 1)

    for copy in t_copies:
        copy.wait_recv()
    group = npeer * nz

    def build_own(o, _):
        table = trecv[...].reshape(group, 128)
        high = (table // 16).astype(F32).astype(BF16)
        low = (table % 16).astype(F32).astype(BF16)
        lane = lax.broadcasted_iota(jnp.int32, (128, slots), 1)
        take = lax.broadcasted_iota(jnp.int32, (128, slots), 0)
        pick = jnp.where(take == o * SLOTS + lane % SLOTS, 1.0, 0.0).astype(BF16)
        spread = nn(high, pick) * 16.0 + nn(low, pick)
        which = lax.broadcasted_iota(jnp.int32, (group, slots), 0)
        at = lax.broadcasted_iota(jnp.int32, (group, slots), 1) // SLOTS
        row = jnp.sum(jnp.where(which == at, spread, 0.0), axis=0, keepdims=True).astype(jnp.int32)
        for c in range(rows // 128):
            ids = lax.broadcasted_iota(jnp.int32, (128, slots), 0) + c * 128
            onehot_own[o, c * 128 : (c + 1) * 128, :] = jnp.where(ids == row, 1.0, 0.0).astype(BF16)
        return 0

    lax.fori_loop(0, nz, build_own, 0)

    def allowed_of(o):
        lengths = hist[o, 0:1, :]
        line = lax.broadcasted_iota(jnp.int32, (rows, 1), 0)
        end = jnp.zeros((1, 1), jnp.int32)
        start = jnp.zeros((rows, 1), jnp.int32)
        for h in range(8):
            length = lengths[:, h : h + 1]
            end = end + length
            start = start + jnp.where(line >= end, length, 0)
        i = lax.broadcasted_iota(jnp.int32, (rows, rows), 0)
        j = lax.broadcasted_iota(jnp.int32, (rows, rows), 1)
        return (j <= i) & (j >= start)

    def weigh(o, _):
        scores = nt(own[0, o], own[1, o]) * scale
        sig = 0.5 * jnp.tanh(0.5 * scores) + 0.5
        weights = jnp.where(allowed_of(o), scores * sig, 0.0).astype(BF16)
        wbuf[o, :, 0:rows] = weights[0:half]
        wbuf[o, :, rows:] = weights[half:]
        return 0

    def weights_of(o):
        return jnp.concatenate([wbuf[o, :, 0:rows], wbuf[o, :, rows:]], axis=0)

    def attend(o, _):
        att = nn(weights_of(o), own[2, o]).astype(BF16)
        att_own[o] = att
        moved = tn(att, onehot_own[o]).astype(BF16).T
        xsend[0, :, o] = moved.reshape(npeer, nz, SLOTS, HEAD)
        return 0

    def sent_in(u):
        block_wait(xsend.at[u, 1:npeer], xin_s.at[u])

    for i in range(2, 5):
        pack_in(0, i)
    pack_in(1, 1)
    pack_in(1, 2)

    w_local.wait()
    for copy in w_copies:
        copy.wait_recv()

    def dz_block(i, _):
        r = pl.ds(pl.multiple_of(i * 128, 128), 128)
        cot = cot_ref[r, :]
        for j in range(ny):
            c = slice(j * wrows, (j + 1) * wrows)
            gg_ref[r, c] = (nt(cot, wfull[j]) * gates_ref[r, c].astype(F32)).astype(BF16)
        return 0

    lax.fori_loop(0, rows // 128, dz_block, 0)
    z_in(3, gg_ref)

    unpack_in(0)
    pack_in(1, 3)
    pack_in(1, 4)
    pack_in(3, 0)
    pack_in(2, 1)
    pack_in(2, 2)
    unpack_in(1)
    pack_in(2, 3)
    lax.fori_loop(0, nz // 2, weigh, 0)
    pack_in(2, 4)
    lax.fori_loop(nz // 2, nz, weigh, 0)
    pack_in(3, 1)
    pack_in(3, 2)
    unpack_in(2)
    pack_in(3, 3)
    sent_in(0)
    lax.fori_loop(0, nz // 2, attend, 0)
    pack_in(3, 4)
    lax.fori_loop(nz // 2, nz, attend, 0)

    into = (0, 1, 2, 4)

    def x_out(u, parts=(3, 2, 1, 0), owners=slice(0, nz)):
        for i in parts:
            places = slice(*groups[i])
            for d in range(1, npeer):
                to = ppeer(d)
                remote(
                    xsend.at[u, to, owners, places], xrecv.at[into[u], p, owners, places],
                    xo_s.at[u], xo_r.at[u, i], pdev(to),
                )
            pltpu.make_async_copy(
                xsend.at[u, p, owners, places], xrecv.at[into[u], p, owners, places],
                xo_r.at[u, i],
            ).start()

    def back(u, dst, i):
        lo, hi = groups[i]
        block_wait(xrecv.at[into[u], :, :, lo:hi], xo_r.at[u, i])

        def tokens(j, _):
            got = xrecv[into[u], :, :, j].reshape(slots, HEAD)
            zbuf[u, j] = tn(got, onehot_src[j]).astype(BF16).T
            return 0

        lax.fori_loop(lo, hi, tokens, 0)
        for j in range(lo, hi):
            if j == 0:
                pltpu.make_async_copy(zbuf.at[u, 0], dst.at[:, columns(z)], zo_r.at[u]).start()
            else:
                remote(
                    zbuf.at[u, j], dst.at[:, columns(z)], zo_s.at[u], zo_r.at[u],
                    zdev(zpeer(nz - order[j])),
                )

    x_out(0, (3, 0, 1, 2))

    block_wait(xrecv.at[3], xin_r.at[3])

    def stats(o, _):
        moved = nn(onehot_own[o], xrecv[3, :, o].reshape(slots, HEAD)).astype(BF16)
        own[3, o] = moved
        att = att_own[o].astype(F32)
        dz = moved.astype(F32)
        mean = jnp.sum(att, axis=1, keepdims=True) * (1.0 / HEAD)
        cent = att - mean
        second = jnp.sum(cent * cent, axis=1, keepdims=True)
        total = jnp.sum(dz, axis=1, keepdims=True)
        cross = jnp.sum(dz * cent, axis=1, keepdims=True)
        lane = lax.broadcasted_iota(jnp.int32, (rows, HEAD), 1)
        table = jnp.where(
            lane == 0, mean, jnp.where(lane == 1, second, jnp.where(lane == 2, total, cross))
        )
        stat_s[o] = table.T[0:8, :]
        return 0

    lax.fori_loop(0, nz // 2, stats, 0)
    back(0, att_full, 3)
    lax.fori_loop(nz // 2, nz, stats, 0)
    sa_copies = [
        remote(stat_s.at[zpeer(d)], stat_r.at[z], sa_s.at[d], sa_r.at[d], zdev(zpeer(d)))
        for d in range(1, nz)
    ]
    stat_r[z] = stat_s[z]
    for copy in sa_copies:
        copy.wait_recv()
    features = float(nz * HEAD)
    got = stat_r[...]
    means, seconds, totals, crosses = [got[:, i : i + 1, :] for i in range(4)]
    mean = jnp.sum(means, axis=0) * (1.0 / nz)
    shift = means - mean[None]
    var = (jnp.sum(seconds, axis=0) + HEAD * jnp.sum(shift * shift, axis=0)) / features
    inverse = lax.rsqrt(var + EPSILON)
    mean_grad = jnp.sum(totals, axis=0) / features
    mean_cross = jnp.sum(crosses + shift * totals, axis=0) * inverse / features
    stat_f[z] = jnp.concatenate([mean, inverse, mean_grad, mean_cross] * 2, axis=0)
    sb_copies = [
        remote(stat_f.at[z], stat_f.at[z], sb_s.at[d], sb_r.at[d], zdev(zpeer(d)))
        for d in range(1, nz)
    ]
    back(0, att_full, 0)
    back(0, att_full, 1)
    for u in range(1, 4):
        sent_in(u)
    for copy in sb_copies:
        copy.wait_recv()

    def value_grads(o, _):
        full = jnp.concatenate([stat_f[o]] * (HEAD // 8), axis=0).T
        mean, inverse = full[:, 0:1], full[:, 1:2]
        mean_grad, mean_cross = full[:, 2:3], full[:, 3:4]
        normed = (att_own[o].astype(F32) - mean) * inverse
        grad = (own[3, o].astype(F32) - mean_grad - normed * mean_cross) * inverse
        grad = grad.astype(BF16)
        own[3, o] = grad
        gv_t = tn(grad, weights_of(o)).astype(BF16)
        xsend[1, :, o] = nn(gv_t, onehot_own[o]).astype(BF16).T.reshape(npeer, nz, SLOTS, HEAD)
        return 0

    def score_grads(o, _):
        q, k, v, grad = own[0, o], own[1, o], own[2, o], own[3, o]
        scores = nt(q, k) * scale
        sig = 0.5 * jnp.tanh(0.5 * scores) + 0.5
        slope = sig + scores * sig * (1.0 - sig)
        gs = jnp.where(allowed_of(o), nt(grad, v) * slope * scale, 0.0).astype(BF16)
        gq_t = nn(gs, k).astype(BF16)
        gk_t = tn(q, gs).astype(BF16)
        spots = onehot_own[o]
        xsend[2, :, o] = tn(gq_t, spots).astype(BF16).T.reshape(npeer, nz, SLOTS, HEAD)
        xsend[3, :, o] = nn(gk_t, spots).astype(BF16).T.reshape(npeer, nz, SLOTS, HEAD)
        return 0

    lax.fori_loop(0, nz // 2, value_grads, 0)
    back(0, att_full, 2)
    lax.fori_loop(nz // 2, nz, value_grads, 0)
    x_out(1)
    lax.fori_loop(0, 4, score_grads, 0)
    for u in range(4):
        block_wait(zbuf.at[u, 1:nz], zin_s.at[u])
    back(1, gv_ref, 3)
    lax.fori_loop(4, 6, score_grads, 0)

    block_wait(att_full, zo_r.at[0])

    def final_block(i, _):
        r = pl.ds(pl.multiple_of(i * 128, 128), 128)
        att = att_full[r, :].astype(F32)
        cent = att - jnp.mean(att, axis=1, keepdims=True)
        inv = lax.rsqrt(jnp.mean(cent * cent, axis=1, keepdims=True) + EPSILON)
        normed = cent * inv
        gated = (normed * gates_ref[r, :].astype(F32)).astype(BF16)
        att_full[r, :] = gated
        cot = cot_ref[r, :]
        acc = None
        for j in range(ny):
            c = slice(j * wrows, (j + 1) * wrows)
            gg_ref[r, c] = (nt(cot, wfull[j]) * normed[:, c]).astype(BF16)
            step = nn(gated[:, c], wfull[j])
            acc = step if acc is None else acc + step
        out_ref[r, :] = acc.astype(BF16)
        return 0

    lax.fori_loop(0, rows // 128, final_block, 0)
    out_copy = pltpu.make_async_copy(out_ref, out_to, loc.at[1])
    out_copy.start()
    gg_copy = pltpu.make_async_copy(gg_ref, gg_to, loc.at[2])
    gg_copy.start()

    def weight_block(j, _):
        c = pl.ds(pl.multiple_of(j * wrows, wrows), wrows)
        wbuf[j] = tn(att_full[:, c], cot_ref[...]).astype(BF16)
        return 0

    lax.fori_loop(0, ny, weight_block, 0)
    core = lax.rem(p, 2)
    chip = lax.div(p, 2)
    chips = npeer // 2
    mine = pl.ds(pl.multiple_of(core * (wrows // 2), wrows // 2), wrows // 2)
    theirs = pl.ds(pl.multiple_of((1 - core) * (wrows // 2), wrows // 2), wrows // 2)
    pair = remote(
        wbuf.at[0:ny, theirs], pair_recv, pr_s.at[0], pr_r.at[0], pdev(chip * 2 + 1 - core)
    )
    back(1, gv_ref, 2)
    lax.fori_loop(6, nz, score_grads, 0)
    x_out(2, (3, 2, 1))
    pair.wait_recv()

    def sum_pair(j, _):
        wbuf[j, mine] = (wbuf[j, mine].astype(F32) + pair_recv[j].astype(F32)).astype(BF16)
        return 0

    lax.fori_loop(0, ny, sum_pair, 0)
    dy_copies = [
        remote(wbuf.at[ypeer(d), mine], dw_recv.at[y], dy_s.at[d], dy_r.at[d], ydev(ypeer(d)))
        for d in range(1, ny)
    ]
    dw_recv[y] = wbuf[y, mine]
    back(1, gv_ref, 1)
    back(1, gv_ref, 0)
    back(2, gq_ref, 3)
    back(2, gq_ref, 2)

    for copy in dy_copies:
        copy.wait_recv()

    def sum_y(j, _):
        r = pl.ds(pl.multiple_of(j * part, part), part)
        acc = dw_recv[0, r, :].astype(F32)
        for i in range(1, ny):
            acc = acc + dw_recv[i, r, :].astype(F32)
        r1_send[j] = acc.astype(BF16)
        return 0

    lax.fori_loop(0, chips, sum_y, 0)
    dp_copies = []
    for d in range(1, chips):
        to = lax.rem(chip + d, chips)
        dp_copies.append(
            remote(
                r1_send.at[to], r1_recv.at[chip], dp_s.at[d], dp_r.at[d], pdev(to * 2 + core)
            )
        )
    r1_recv[chip] = r1_send[chip]
    x_out(2, (0,))
    x_out(3)
    for copy in dp_copies:
        copy.wait_recv()
    acc = r1_recv[0].astype(F32)
    for i in range(1, chips):
        acc = acc + r1_recv[i].astype(F32)
    for i in range(nz):
        r2_send[i] = acc[:, i * HEAD : (i + 1) * HEAD].astype(BF16)
    dz_copies = [
        remote(r2_send.at[zpeer(d)], r2_recv.at[z], dz_s.at[d], dz_r.at[d], zdev(zpeer(d)))
        for d in range(1, nz)
    ]
    r2_recv[z] = r2_send[z]
    back(2, gq_ref, 1)
    back(2, gq_ref, 0)
    for copy in dz_copies:
        copy.wait_recv()
    acc = r2_recv[0].astype(F32)
    for i in range(1, nz):
        acc = acc + r2_recv[i].astype(F32)
    gz[z] = acc.astype(BF16)
    az_copies = [
        remote(gz.at[z], gz.at[z], az_s.at[d], az_r.at[d], zdev(zpeer(d))) for d in range(1, nz)
    ]
    back(3, gk_ref, 3)
    back(3, gk_ref, 2)
    back(3, gk_ref, 1)
    for copy in az_copies:
        copy.wait_recv()
    place = core * chips + chip
    gw_ref[place] = jnp.concatenate([gz[i] for i in range(nz)], axis=1)
    ap_copies = [
        remote(gw_ref.at[place], gw_ref.at[place], ap_s.at[d], ap_r.at[d], pdev(ppeer(d)))
        for d in range(1, npeer)
    ]
    back(3, gk_ref, 0)
    for copy in ap_copies:
        copy.wait_recv()

    out_copy.wait()
    gg_copy.wait()
    for u, dst in ((1, gv_ref), (2, gq_ref), (3, gk_ref)):
        block_wait(dst, zo_r.at[u])
    for u in range(4):
        block_wait(zbuf.at[u, 1:nz], zo_s.at[u])
        block_wait(xsend.at[u, 1:npeer], xo_s.at[u])
    for copies in (
        meta_copies, w_copies, t_copies, sa_copies, sb_copies,
        [pair], dy_copies, dp_copies, dz_copies, az_copies, ap_copies,
    ):
        for copy in copies:
            copy.wait_send()


def settle(*refs):
    sources, targets, held, sems = refs[:6], refs[6:12], refs[12:18], refs[18]
    wide = refs[19]
    loads = [
        pltpu.make_async_copy(src, buf, sems.at[i])
        for i, (src, buf) in enumerate(zip(sources, held))
    ]
    for copy in loads:
        copy.start()
    stores = []
    for i in range(5):
        loads[i].wait()
        stores.append(pltpu.make_async_copy(held[i], targets[i], sems.at[6 + i]))
        stores[i].start()
    loads[5].wait()
    wide[...] = held[5][...].reshape(wide.shape).astype(F32)
    stores.append(pltpu.make_async_copy(wide, targets[5], sems.at[11]))
    stores[5].start()
    for copy in stores:
        copy.wait()


def body(nz, npeer, ny, queries, keys, values, gates, cotangent, hist_len, token_owner, token_row, w_out):
    rows, width = queries.shape
    slots = nz * npeer * SLOTS
    wrows = w_out.shape[0]
    part = wrows // npeer
    dma = pltpu.SemaphoreType.DMA
    vmem = pl.BlockSpec(memory_space=pltpu.VMEM)
    anywhere = pl.BlockSpec(memory_space=pl.ANY)
    wide = jax.ShapeDtypeStruct((rows, width), BF16)
    out = pl.pallas_call(
        functools.partial(kernel, nz, npeer, ny),
        out_shape=(
            wide, wide, wide, wide, wide,
            jax.ShapeDtypeStruct((npeer, part, width), BF16),
        ),
        in_specs=[anywhere, anywhere, anywhere, vmem, vmem, vmem, vmem, vmem, anywhere],
        out_specs=(anywhere, anywhere, anywhere, anywhere, anywhere, vmem),
        scratch_shapes=[
            pltpu.VMEM((rows, width), BF16),
            pltpu.VMEM((rows, width), BF16),
            pltpu.VMEM((nz, slots, rows), BF16),
            pltpu.VMEM((nz, rows, slots), BF16),
            pltpu.VMEM((4, nz, rows, HEAD), BF16),
            pltpu.VMEM((4, npeer, nz, nz, SLOTS, HEAD), BF16),
            pltpu.VMEM((5, npeer, nz, nz, SLOTS, HEAD), BF16),
            pltpu.VMEM((4, nz, rows, HEAD), BF16),
            pltpu.VMEM((nz, rows, HEAD), BF16),
            pltpu.VMEM((nz, rows // 2, 2 * rows), BF16),
            pltpu.VMEM((ny, wrows, width), BF16),
            pltpu.VMEM((rows, width), BF16),
            pltpu.VMEM((nz, 8, META), jnp.int32),
            pltpu.VMEM((nz, 8, 128), jnp.int32),
            pltpu.VMEM((npeer, nz, 128), jnp.int32),
            pltpu.VMEM((npeer, nz, 128), jnp.int32),
            pltpu.VMEM((nz, 8, rows), F32),
            pltpu.VMEM((nz, 8, rows), F32),
            pltpu.VMEM((nz, 8, rows), F32),
            pltpu.VMEM((ny, wrows // 2, width), BF16),
            pltpu.VMEM((ny, wrows // 2, width), BF16),
            pltpu.VMEM((npeer // 2, part, width), BF16),
            pltpu.VMEM((npeer // 2, part, width), BF16),
            pltpu.VMEM((nz, part, HEAD), BF16),
            pltpu.VMEM((nz, part, HEAD), BF16),
            pltpu.VMEM((nz, part, HEAD), BF16),
            dma((3,)),
            dma((4,)), dma((4, nz)),
            dma((4,)), dma((4,)),
            dma((4,)), dma((4, 4)),
            dma((4,)), dma((4,)),
            dma((nz,)), dma((nz,)),
            dma((npeer,)), dma((npeer,)),
            dma((ny,)), dma((ny,)),
            dma((nz,)), dma((nz,)),
            dma((nz,)), dma((nz,)),
            dma((1,)), dma((1,)),
            dma((ny,)), dma((ny,)),
            dma((npeer // 2,)), dma((npeer // 2,)),
            dma((nz,)), dma((nz,)),
            dma((nz,)), dma((nz,)),
            dma((npeer,)), dma((npeer,)),
        ],
        compiler_params=pltpu.CompilerParams(
            collective_id=0, has_side_effects=True, vmem_limit_bytes=63 * 1024 * 1024
        ),
    )(
        queries, keys, values, gates, cotangent,
        token_owner.reshape(1, rows), token_row.reshape(1, rows), hist_len, w_out,
    )
    out, gq, gk, gv, gg, gw = out
    hbm = pl.BlockSpec(memory_space=pltpu.HBM)
    whole = jax.ShapeDtypeStruct((wrows, width), F32)
    gk, gq, gv, out, gg, gw = pl.pallas_call(
        settle,
        out_shape=(wide,) * 5 + (whole,),
        in_specs=[hbm] * 6,
        out_specs=(hbm,) * 6,
        scratch_shapes=[pltpu.VMEM((rows, width), BF16)] * 5
        + [pltpu.VMEM((npeer, part, width), BF16), dma((12,)), pltpu.VMEM((wrows, width), F32)],
        compiler_params=pltpu.CompilerParams(vmem_limit_bytes=60 * 1024 * 1024),
    )(gk, gq, gv, out, gg, gw)
    return out, gq, gk, gv, gg, gw


def solution(mesh):
    ny = mesh.shape["dp"]
    nz = 8
    npeer = mesh.shape["bal"] // nz
    token = P(("dp", "bal"))
    wide = P(("dp", "bal"), None)
    return jax.shard_map(
        functools.partial(body, nz, npeer, ny),
        mesh=mesh,
        in_specs=(wide, wide, wide, wide, wide, wide, token, token, P("dp", None)),
        out_specs=(wide, wide, wide, wide, wide, P("dp", None)),
        check_vma=False,
    )
```

```python
import functools
import math

import jax
import jax.numpy as jnp
from jax import lax
from jax.experimental import pallas as pl
from jax.experimental.pallas import tpu as pltpu
from jax.sharding import PartitionSpec as P

HEAD = 128
EPSILON = 1e-05
SLOTS = 16
MESH = pl.DeviceIdType.MESH
F32 = jnp.float32
BF16 = jnp.bfloat16
META = 768


def nn(a, b):
    return lax.dot_general(a, b, (((1,), (0,)), ((), ())), preferred_element_type=F32)


def nt(a, b):
    return lax.dot_general(a, b, (((1,), (1,)), ((), ())), preferred_element_type=F32)


def tn(a, b):
    return lax.dot_general(a, b, (((0,), (0,)), ((), ())), preferred_element_type=F32)


def block_wait(ref, sem):
    pltpu.make_async_copy(ref, ref, sem).wait()


def kernel(
    nz, npeer, ny,
    q_ref, k_ref, v_ref, gates_ref, cot_ref, owner_ref, row_ref, len_ref, w_ref,
    out_to, gq_ref, gk_ref, gv_ref, gg_to, gw_ref,
    out_ref, gg_ref, onehot_src, onehot_own, zbuf, xsend, xrecv, own, att_own, wbuf, wfull, att_full,
    metaz, hist, tsend, trecv, stat_s, stat_r, stat_f,
    pair_recv, dw_recv, r1_send, r1_recv, r2_send, r2_recv, gz,
    loc, zin_s, zin_r, xin_s, xin_r, xo_s, xo_r, zo_s, zo_r,
    m_s, m_r, t_s, t_r, w_s, w_r, sa_s, sa_r, sb_s, sb_r,
    pr_s, pr_r, dy_s, dy_r, dp_s, dp_r, dz_s, dz_r, az_s, az_r, ap_s, ap_r,
):
    y = lax.axis_index("dp")
    b = lax.axis_index("bal")
    z = b // npeer
    p = lax.rem(b, npeer)
    rows = q_ref.shape[0]
    wrows = wfull.shape[1]
    part = wrows // npeer
    half = rows // 2
    slots = npeer * nz * SLOTS
    scale = 1.0 / math.sqrt(HEAD)
    order = [0]
    for d in range(1, nz // 2 + 1):
        order += [d, nz - d] if 2 * d < nz else [d]
    bounds = (0, 1, 3, 5, 7, 8)
    groups = ((0, 3), (3, 5), (5, 7), (7, 8))

    def zpeer(d):
        return lax.rem(z + d, nz)

    def ppeer(d):
        return lax.rem(p + d, npeer)

    def ypeer(d):
        return lax.rem(y + d, ny)

    def zdev(at):
        return (y, at * npeer + p)

    def pdev(at):
        return (y, z * npeer + at)

    def ydev(at):
        return (at, b)

    def columns(at):
        return pl.ds(pl.multiple_of(at * HEAD, HEAD), HEAD)

    def remote(src, dst, ssem, rsem, device):
        copy = pltpu.make_async_remote_copy(
            src_ref=src, dst_ref=dst, send_sem=ssem, recv_sem=rsem,
            device_id=device, device_id_type=MESH,
        )
        copy.start()
        return copy

    barrier = pltpu.get_barrier_semaphore()
    for d in range(1, nz):
        pl.semaphore_signal(barrier, inc=1, device_id=zdev(zpeer(d)), device_id_type=MESH)
    for d in range(1, npeer):
        pl.semaphore_signal(barrier, inc=1, device_id=pdev(ppeer(d)), device_id_type=MESH)
    for d in range(1, ny):
        pl.semaphore_signal(barrier, inc=1, device_id=ydev(ypeer(d)), device_id_type=MESH)

    owner = owner_ref[...]
    column = jnp.broadcast_to(owner.astype(F32), (128, rows)).T[:, 0:1]
    first = lax.broadcasted_iota(jnp.int32, (rows, rows), 0)
    second = lax.broadcasted_iota(jnp.int32, (rows, rows), 1)
    same = (column == owner.astype(F32)) & (first < second)
    rank = jnp.sum(jnp.where(same, 1.0, 0.0), axis=0, keepdims=True).astype(jnp.int32)
    slot = lax.rem(owner, npeer) * (nz * SLOTS) + lax.div(owner, npeer) * SLOTS + rank
    metaz[0, :, 0:rows] = jnp.broadcast_to(slot, (8, rows))

    def build_src(i, _):
        slot = metaz[i, 0:1, 0:rows]
        for c in range(slots // 128):
            ids = lax.broadcasted_iota(jnp.int32, (128, rows), 0) + c * 128
            onehot_src[i, c * 128 : (c + 1) * 128, :] = jnp.where(ids == slot, 1.0, 0.0).astype(BF16)
        return 0

    build_src(0, 0)
    token_row = jnp.broadcast_to(row_ref[...], (8, rows))
    line = lax.broadcasted_iota(jnp.int32, (8, rows), 0)
    digits = jnp.where(
        line == 0, lax.div(token_row, 16), jnp.where(line == 1, lax.rem(token_row, 16), 1)
    )
    found = nt(digits.astype(F32).astype(BF16), onehot_src[0])
    row_of = found[0:1] * 16.0 + found[1:2] + (1.0 - found[2:3]) * rows
    row_of = row_of.astype(jnp.int32)
    metaz[0, :, 512:640] = jnp.concatenate(
        [row_of[:, i * nz * SLOTS : (i + 1) * nz * SLOTS] for i in range(npeer)], axis=0
    )
    metaz[0, :, 640:648] = jnp.broadcast_to(len_ref[...], (8, 8))

    pl.semaphore_wait(barrier, nz + npeer + ny - 3)

    meta_copies = [
        remote(metaz.at[0], metaz.at[j], m_s.at[j], m_r.at[j], zdev(zpeer(order[j])))
        for j in range(1, nz)
    ]
    def z_in(u, src):
        pltpu.make_async_copy(src.at[:, columns(z)], zbuf.at[u, 0], zin_r.at[u, 0]).start()
        for j in range(1, nz):
            to = zpeer(order[j])
            remote(src.at[:, columns(to)], zbuf.at[u, j], zin_s.at[u], zin_r.at[u, j], zdev(to))

    z_in(0, q_ref)
    w_copies = [
        remote(w_ref, wfull.at[y], w_s.at[d], w_r.at[d], ydev(ypeer(d))) for d in range(1, ny)
    ]
    w_local = pltpu.make_async_copy(w_ref, wfull.at[y], loc.at[0])
    w_local.start()
    z_in(1, k_ref)
    z_in(2, v_ref)
    def pack_in(u, i):
        lo, hi = bounds[i], bounds[i + 1]
        places = slice(lo, hi)

        def step(j, _):
            block_wait(zbuf.at[u, j], zin_r.at[u, j])
            moved = nn(onehot_src[j], zbuf[u, j]).astype(BF16)
            xsend[u, :, :, j] = moved.reshape(npeer, nz, SLOTS, HEAD)
            return 0

        lax.fori_loop(lo, hi, step, 0)
        for d in range(1, npeer):
            to = ppeer(d)
            remote(
                xsend.at[u, to, :, places], xrecv.at[u, p, :, places], xin_s.at[u], xin_r.at[u],
                pdev(to),
            )
        if hi == nz:
            pltpu.make_async_copy(xsend.at[u, p], xrecv.at[u, p], xin_r.at[u]).start()

    def unpack_in(u):
        block_wait(xrecv.at[u], xin_r.at[u])

        def step(o, _):
            own[u, o] = nn(onehot_own[o], xrecv[u, :, o].reshape(slots, HEAD)).astype(BF16)
            return 0

        lax.fori_loop(0, nz, step, 0)

    for u in range(3):
        pack_in(u, 0)

    for copy in meta_copies:
        copy.wait_recv()
    for j in range(nz):
        hist[zpeer(nz - order[j])] = metaz[j, :, 640:768]
    for at in range(npeer):
        tsend[at] = metaz[:, at, 512:640]
    t_copies = [
        remote(tsend.at[ppeer(d)], trecv.at[p], t_s.at[d], t_r.at[d], pdev(ppeer(d)))
        for d in range(1, npeer)
    ]
    trecv[p] = tsend[p]
    lax.fori_loop(1, nz, build_src, 0)

    pack_in(0, 1)

    for copy in t_copies:
        copy.wait_recv()
    group = npeer * nz

    def build_own(o, _):
        table = trecv[...].reshape(group, 128)
        high = (table // 16).astype(F32).astype(BF16)
        low = (table % 16).astype(F32).astype(BF16)
        lane = lax.broadcasted_iota(jnp.int32, (128, slots), 1)
        take = lax.broadcasted_iota(jnp.int32, (128, slots), 0)
        pick = jnp.where(take == o * SLOTS + lane % SLOTS, 1.0, 0.0).astype(BF16)
        spread = nn(high, pick) * 16.0 + nn(low, pick)
        which = lax.broadcasted_iota(jnp.int32, (group, slots), 0)
        at = lax.broadcasted_iota(jnp.int32, (group, slots), 1) // SLOTS
        row = jnp.sum(jnp.where(which == at, spread, 0.0), axis=0, keepdims=True).astype(jnp.int32)
        for c in range(rows // 128):
            ids = lax.broadcasted_iota(jnp.int32, (128, slots), 0) + c * 128
            onehot_own[o, c * 128 : (c + 1) * 128, :] = jnp.where(ids == row, 1.0, 0.0).astype(BF16)
        return 0

    lax.fori_loop(0, nz, build_own, 0)

    def allowed_of(o):
        lengths = hist[o, 0:1, :]
        line = lax.broadcasted_iota(jnp.int32, (rows, 1), 0)
        end = jnp.zeros((1, 1), jnp.int32)
        start = jnp.zeros((rows, 1), jnp.int32)
        for h in range(8):
            length = lengths[:, h : h + 1]
            end = end + length
            start = start + jnp.where(line >= end, length, 0)
        i = lax.broadcasted_iota(jnp.int32, (rows, rows), 0)
        j = lax.broadcasted_iota(jnp.int32, (rows, rows), 1)
        return (j <= i) & (j >= start)

    def weigh(o, _):
        scores = nt(own[0, o], own[1, o]) * scale
        sig = 0.5 * jnp.tanh(0.5 * scores) + 0.5
        weights = jnp.where(allowed_of(o), scores * sig, 0.0).astype(BF16)
        wbuf[o, :, 0:rows] = weights[0:half]
        wbuf[o, :, rows:] = weights[half:]
        return 0

    def weights_of(o):
        return jnp.concatenate([wbuf[o, :, 0:rows], wbuf[o, :, rows:]], axis=0)

    def attend(o, _):
        att = nn(weights_of(o), own[2, o]).astype(BF16)
        att_own[o] = att
        moved = tn(att, onehot_own[o]).astype(BF16).T
        xsend[0, :, o] = moved.reshape(npeer, nz, SLOTS, HEAD)
        return 0

    def sent_in(u):
        block_wait(xsend.at[u, 1:npeer], xin_s.at[u])

    for i in range(2, 5):
        pack_in(0, i)
    pack_in(1, 1)
    pack_in(1, 2)

    w_local.wait()
    for copy in w_copies:
        copy.wait_recv()

    def dz_block(i, _):
        r = pl.ds(pl.multiple_of(i * 128, 128), 128)
        cot = cot_ref[r, :]
        for j in range(ny):
            c = slice(j * wrows, (j + 1) * wrows)
            gg_ref[r, c] = (nt(cot, wfull[j]) * gates_ref[r, c].astype(F32)).astype(BF16)
        return 0

    lax.fori_loop(0, rows // 128, dz_block, 0)
    z_in(3, gg_ref)

    unpack_in(0)
    pack_in(1, 3)
    pack_in(1, 4)
    pack_in(3, 0)
    pack_in(2, 1)
    pack_in(2, 2)
    unpack_in(1)
    pack_in(2, 3)
    lax.fori_loop(0, nz // 2, weigh, 0)
    pack_in(2, 4)
    lax.fori_loop(nz // 2, nz, weigh, 0)
    pack_in(3, 1)
    pack_in(3, 2)
    unpack_in(2)
    sent_in(0)
    lax.fori_loop(0, nz // 2, attend, 0)
    pack_in(3, 3)
    pack_in(3, 4)
    lax.fori_loop(nz // 2, nz, attend, 0)

    into = (0, 1, 2, 4)

    def x_out(u, parts=(3, 2, 1, 0), owners=slice(0, nz)):
        for i in parts:
            places = slice(*groups[i])
            for d in range(1, npeer):
                to = ppeer(d)
                remote(
                    xsend.at[u, to, owners, places], xrecv.at[into[u], p, owners, places],
                    xo_s.at[u], xo_r.at[u, i], pdev(to),
                )
            pltpu.make_async_copy(
                xsend.at[u, p, owners, places], xrecv.at[into[u], p, owners, places],
                xo_r.at[u, i],
            ).start()

    def back(u, dst, i):
        lo, hi = groups[i]
        block_wait(xrecv.at[into[u], :, :, lo:hi], xo_r.at[u, i])

        def tokens(j, _):
            got = xrecv[into[u], :, :, j].reshape(slots, HEAD)
            zbuf[u, j] = tn(got, onehot_src[j]).astype(BF16).T
            return 0

        lax.fori_loop(lo, hi, tokens, 0)
        for j in range(lo, hi):
            if j == 0:
                pltpu.make_async_copy(zbuf.at[u, 0], dst.at[:, columns(z)], zo_r.at[u]).start()
            else:
                remote(
                    zbuf.at[u, j], dst.at[:, columns(z)], zo_s.at[u], zo_r.at[u],
                    zdev(zpeer(nz - order[j])),
                )

    x_out(0, (0, 1, 3, 2))

    block_wait(xrecv.at[3], xin_r.at[3])

    def stats(o, _):
        moved = nn(onehot_own[o], xrecv[3, :, o].reshape(slots, HEAD)).astype(BF16)
        own[3, o] = moved
        att = att_own[o].astype(F32)
        dz = moved.astype(F32)
        mean = jnp.sum(att, axis=1, keepdims=True) * (1.0 / HEAD)
        cent = att - mean
        second = jnp.sum(cent * cent, axis=1, keepdims=True)
        total = jnp.sum(dz, axis=1, keepdims=True)
        cross = jnp.sum(dz * cent, axis=1, keepdims=True)
        lane = lax.broadcasted_iota(jnp.int32, (rows, HEAD), 1)
        table = jnp.where(
            lane == 0, mean, jnp.where(lane == 1, second, jnp.where(lane == 2, total, cross))
        )
        stat_s[o] = table.T[0:8, :]
        return 0

    lax.fori_loop(0, nz, stats, 0)
    sa_copies = [
        remote(stat_s.at[zpeer(d)], stat_r.at[z], sa_s.at[d], sa_r.at[d], zdev(zpeer(d)))
        for d in range(1, nz)
    ]
    stat_r[z] = stat_s[z]
    for copy in sa_copies:
        copy.wait_recv()
    features = float(nz * HEAD)
    got = stat_r[...]
    means, seconds, totals, crosses = [got[:, i : i + 1, :] for i in range(4)]
    mean = jnp.sum(means, axis=0) * (1.0 / nz)
    shift = means - mean[None]
    var = (jnp.sum(seconds, axis=0) + HEAD * jnp.sum(shift * shift, axis=0)) / features
    inverse = lax.rsqrt(var + EPSILON)
    mean_grad = jnp.sum(totals, axis=0) / features
    mean_cross = jnp.sum(crosses + shift * totals, axis=0) * inverse / features
    stat_f[z] = jnp.concatenate([mean, inverse, mean_grad, mean_cross] * 2, axis=0)
    sb_copies = [
        remote(stat_f.at[z], stat_f.at[z], sb_s.at[d], sb_r.at[d], zdev(zpeer(d)))
        for d in range(1, nz)
    ]
    back(0, att_full, 0)
    for u in range(1, 4):
        sent_in(u)
    for copy in sb_copies:
        copy.wait_recv()

    def value_grads(o, _):
        full = jnp.concatenate([stat_f[o]] * (HEAD // 8), axis=0).T
        mean, inverse = full[:, 0:1], full[:, 1:2]
        mean_grad, mean_cross = full[:, 2:3], full[:, 3:4]
        normed = (att_own[o].astype(F32) - mean) * inverse
        grad = (own[3, o].astype(F32) - mean_grad - normed * mean_cross) * inverse
        grad = grad.astype(BF16)
        own[3, o] = grad
        gv_t = tn(grad, weights_of(o)).astype(BF16)
        xsend[1, :, o] = nn(gv_t, onehot_own[o]).astype(BF16).T.reshape(npeer, nz, SLOTS, HEAD)
        return 0

    def score_grads(o, _):
        q, k, v, grad = own[0, o], own[1, o], own[2, o], own[3, o]
        scores = nt(q, k) * scale
        sig = 0.5 * jnp.tanh(0.5 * scores) + 0.5
        slope = sig + scores * sig * (1.0 - sig)
        gs = jnp.where(allowed_of(o), nt(grad, v) * slope * scale, 0.0).astype(BF16)
        gq_t = nn(gs, k).astype(BF16)
        gk_t = tn(q, gs).astype(BF16)
        spots = onehot_own[o]
        xsend[2, :, o] = tn(gq_t, spots).astype(BF16).T.reshape(npeer, nz, SLOTS, HEAD)
        xsend[3, :, o] = nn(gk_t, spots).astype(BF16).T.reshape(npeer, nz, SLOTS, HEAD)
        return 0

    back(0, att_full, 1)
    lax.fori_loop(0, nz // 2, value_grads, 0)
    back(0, att_full, 3)
    lax.fori_loop(nz // 2, nz, value_grads, 0)
    x_out(1)
    back(0, att_full, 2)
    lax.fori_loop(0, 4, score_grads, 0)
    for u in range(4):
        block_wait(zbuf.at[u, 1:nz], zin_s.at[u])
    back(1, gv_ref, 3)
    lax.fori_loop(4, nz, score_grads, 0)
    x_out(2)
    back(1, gv_ref, 2)
    back(1, gv_ref, 1)

    block_wait(att_full, zo_r.at[0])

    def final_block(i, _):
        r = pl.ds(pl.multiple_of(i * 128, 128), 128)
        att = att_full[r, :].astype(F32)
        cent = att - jnp.mean(att, axis=1, keepdims=True)
        inv = lax.rsqrt(jnp.mean(cent * cent, axis=1, keepdims=True) + EPSILON)
        normed = cent * inv
        gated = (normed * gates_ref[r, :].astype(F32)).astype(BF16)
        att_full[r, :] = gated
        cot = cot_ref[r, :]
        acc = None
        for j in range(ny):
            c = slice(j * wrows, (j + 1) * wrows)
            gg_ref[r, c] = (nt(cot, wfull[j]) * normed[:, c]).astype(BF16)
            step = nn(gated[:, c], wfull[j])
            acc = step if acc is None else acc + step
        out_ref[r, :] = acc.astype(BF16)
        return 0

    lax.fori_loop(0, rows // 128, final_block, 0)
    out_copy = pltpu.make_async_copy(out_ref, out_to, loc.at[1])
    out_copy.start()
    gg_copy = pltpu.make_async_copy(gg_ref, gg_to, loc.at[2])
    gg_copy.start()

    def weight_block(j, _):
        c = pl.ds(pl.multiple_of(j * wrows, wrows), wrows)
        wbuf[j] = tn(att_full[:, c], cot_ref[...]).astype(BF16)
        return 0

    lax.fori_loop(0, ny, weight_block, 0)
    core = lax.rem(p, 2)
    chip = lax.div(p, 2)
    chips = npeer // 2
    mine = pl.ds(pl.multiple_of(core * (wrows // 2), wrows // 2), wrows // 2)
    theirs = pl.ds(pl.multiple_of((1 - core) * (wrows // 2), wrows // 2), wrows // 2)
    pair = remote(
        wbuf.at[0:ny, theirs], pair_recv, pr_s.at[0], pr_r.at[0], pdev(chip * 2 + 1 - core)
    )
    back(1, gv_ref, 0)
    pair.wait_recv()

    def sum_pair(j, _):
        wbuf[j, mine] = (wbuf[j, mine].astype(F32) + pair_recv[j].astype(F32)).astype(BF16)
        return 0

    lax.fori_loop(0, ny, sum_pair, 0)
    dy_copies = [
        remote(wbuf.at[ypeer(d), mine], dw_recv.at[y], dy_s.at[d], dy_r.at[d], ydev(ypeer(d)))
        for d in range(1, ny)
    ]
    dw_recv[y] = wbuf[y, mine]
    back(2, gq_ref, 3)
    back(2, gq_ref, 2)
    back(2, gq_ref, 1)

    for copy in dy_copies:
        copy.wait_recv()

    def sum_y(j, _):
        r = pl.ds(pl.multiple_of(j * part, part), part)
        acc = dw_recv[0, r, :].astype(F32)
        for i in range(1, ny):
            acc = acc + dw_recv[i, r, :].astype(F32)
        r1_send[j] = acc.astype(BF16)
        return 0

    lax.fori_loop(0, chips, sum_y, 0)
    dp_copies = []
    for d in range(1, chips):
        to = lax.rem(chip + d, chips)
        dp_copies.append(
            remote(
                r1_send.at[to], r1_recv.at[chip], dp_s.at[d], dp_r.at[d], pdev(to * 2 + core)
            )
        )
    r1_recv[chip] = r1_send[chip]
    x_out(3)
    back(2, gq_ref, 0)
    for copy in dp_copies:
        copy.wait_recv()
    acc = r1_recv[0].astype(F32)
    for i in range(1, chips):
        acc = acc + r1_recv[i].astype(F32)
    for i in range(nz):
        r2_send[i] = acc[:, i * HEAD : (i + 1) * HEAD].astype(BF16)
    dz_copies = [
        remote(r2_send.at[zpeer(d)], r2_recv.at[z], dz_s.at[d], dz_r.at[d], zdev(zpeer(d)))
        for d in range(1, nz)
    ]
    r2_recv[z] = r2_send[z]
    back(3, gk_ref, 3)
    for copy in dz_copies:
        copy.wait_recv()
    acc = r2_recv[0].astype(F32)
    for i in range(1, nz):
        acc = acc + r2_recv[i].astype(F32)
    gz[z] = acc.astype(BF16)
    az_copies = [
        remote(gz.at[z], gz.at[z], az_s.at[d], az_r.at[d], zdev(zpeer(d))) for d in range(1, nz)
    ]
    back(3, gk_ref, 2)
    back(3, gk_ref, 1)
    back(3, gk_ref, 0)
    for copy in az_copies:
        copy.wait_recv()
    place = core * chips + chip
    gw_ref[place] = jnp.concatenate([gz[i] for i in range(nz)], axis=1)
    ap_copies = [
        remote(gw_ref.at[place], gw_ref.at[place], ap_s.at[d], ap_r.at[d], pdev(ppeer(d)))
        for d in range(1, npeer)
    ]
    for copy in ap_copies:
        copy.wait_recv()

    out_copy.wait()
    gg_copy.wait()
    for u, dst in ((1, gv_ref), (2, gq_ref), (3, gk_ref)):
        block_wait(dst, zo_r.at[u])
    for u in range(4):
        block_wait(zbuf.at[u, 1:nz], zo_s.at[u])
        block_wait(xsend.at[u, 1:npeer], xo_s.at[u])
    for copies in (
        meta_copies, w_copies, t_copies, sa_copies, sb_copies,
        [pair], dy_copies, dp_copies, dz_copies, az_copies, ap_copies,
    ):
        for copy in copies:
            copy.wait_send()


def settle(*refs):
    sources, targets, held, sems = refs[:6], refs[6:12], refs[12:18], refs[18]
    wide = refs[19]
    loads = [
        pltpu.make_async_copy(src, buf, sems.at[i])
        for i, (src, buf) in enumerate(zip(sources, held))
    ]
    for copy in loads:
        copy.start()
    stores = []
    for i in range(5):
        loads[i].wait()
        stores.append(pltpu.make_async_copy(held[i], targets[i], sems.at[6 + i]))
        stores[i].start()
    loads[5].wait()
    wide[...] = held[5][...].reshape(wide.shape).astype(F32)
    stores.append(pltpu.make_async_copy(wide, targets[5], sems.at[11]))
    stores[5].start()
    for copy in stores:
        copy.wait()


def body(nz, npeer, ny, queries, keys, values, gates, cotangent, hist_len, token_owner, token_row, w_out):
    rows, width = queries.shape
    slots = nz * npeer * SLOTS
    wrows = w_out.shape[0]
    part = wrows // npeer
    dma = pltpu.SemaphoreType.DMA
    vmem = pl.BlockSpec(memory_space=pltpu.VMEM)
    anywhere = pl.BlockSpec(memory_space=pl.ANY)
    wide = jax.ShapeDtypeStruct((rows, width), BF16)
    out = pl.pallas_call(
        functools.partial(kernel, nz, npeer, ny),
        out_shape=(
            wide, wide, wide, wide, wide,
            jax.ShapeDtypeStruct((npeer, part, width), BF16),
        ),
        in_specs=[anywhere, anywhere, anywhere, vmem, vmem, vmem, vmem, vmem, anywhere],
        out_specs=(anywhere, anywhere, anywhere, anywhere, anywhere, vmem),
        scratch_shapes=[
            pltpu.VMEM((rows, width), BF16),
            pltpu.VMEM((rows, width), BF16),
            pltpu.VMEM((nz, slots, rows), BF16),
            pltpu.VMEM((nz, rows, slots), BF16),
            pltpu.VMEM((4, nz, rows, HEAD), BF16),
            pltpu.VMEM((4, npeer, nz, nz, SLOTS, HEAD), BF16),
            pltpu.VMEM((5, npeer, nz, nz, SLOTS, HEAD), BF16),
            pltpu.VMEM((4, nz, rows, HEAD), BF16),
            pltpu.VMEM((nz, rows, HEAD), BF16),
            pltpu.VMEM((nz, rows // 2, 2 * rows), BF16),
            pltpu.VMEM((ny, wrows, width), BF16),
            pltpu.VMEM((rows, width), BF16),
            pltpu.VMEM((nz, 8, META), jnp.int32),
            pltpu.VMEM((nz, 8, 128), jnp.int32),
            pltpu.VMEM((npeer, nz, 128), jnp.int32),
            pltpu.VMEM((npeer, nz, 128), jnp.int32),
            pltpu.VMEM((nz, 8, rows), F32),
            pltpu.VMEM((nz, 8, rows), F32),
            pltpu.VMEM((nz, 8, rows), F32),
            pltpu.VMEM((ny, wrows // 2, width), BF16),
            pltpu.VMEM((ny, wrows // 2, width), BF16),
            pltpu.VMEM((npeer // 2, part, width), BF16),
            pltpu.VMEM((npeer // 2, part, width), BF16),
            pltpu.VMEM((nz, part, HEAD), BF16),
            pltpu.VMEM((nz, part, HEAD), BF16),
            pltpu.VMEM((nz, part, HEAD), BF16),
            dma((3,)),
            dma((4,)), dma((4, nz)),
            dma((4,)), dma((4,)),
            dma((4,)), dma((4, 4)),
            dma((4,)), dma((4,)),
            dma((nz,)), dma((nz,)),
            dma((npeer,)), dma((npeer,)),
            dma((ny,)), dma((ny,)),
            dma((nz,)), dma((nz,)),
            dma((nz,)), dma((nz,)),
            dma((1,)), dma((1,)),
            dma((ny,)), dma((ny,)),
            dma((npeer // 2,)), dma((npeer // 2,)),
            dma((nz,)), dma((nz,)),
            dma((nz,)), dma((nz,)),
            dma((npeer,)), dma((npeer,)),
        ],
        compiler_params=pltpu.CompilerParams(
            collective_id=0, has_side_effects=True, vmem_limit_bytes=63 * 1024 * 1024
        ),
    )(
        queries, keys, values, gates, cotangent,
        token_owner.reshape(1, rows), token_row.reshape(1, rows), hist_len, w_out,
    )
    out, gq, gk, gv, gg, gw = out
    hbm = pl.BlockSpec(memory_space=pltpu.HBM)
    whole = jax.ShapeDtypeStruct((wrows, width), F32)
    gk, gq, gv, out, gg, gw = pl.pallas_call(
        settle,
        out_shape=(wide,) * 5 + (whole,),
        in_specs=[hbm] * 6,
        out_specs=(hbm,) * 6,
        scratch_shapes=[pltpu.VMEM((rows, width), BF16)] * 5
        + [pltpu.VMEM((npeer, part, width), BF16), dma((12,)), pltpu.VMEM((wrows, width), F32)],
        compiler_params=pltpu.CompilerParams(vmem_limit_bytes=60 * 1024 * 1024),
    )(gk, gq, gv, out, gg, gw)
    return out, gq, gk, gv, gg, gw


def solution(mesh):
    ny = mesh.shape["dp"]
    nz = 8
    npeer = mesh.shape["bal"] // nz
    token = P(("dp", "bal"))
    wide = P(("dp", "bal"), None)
    return jax.shard_map(
        functools.partial(body, nz, npeer, ny),
        mesh=mesh,
        in_specs=(wide, wide, wide, wide, wide, wide, token, token, P("dp", None)),
        out_specs=(wide, wide, wide, wide, wide, P("dp", None)),
        check_vma=False,
    )
```
